32 devices in a mesh: pulse: 4 (over y, core), tile: 8 (over z, x).
Axes of the slice: x: 2, y: 2, z: 4, core: 2. Of those that a mesh axis runs over, the one named last changes fastest.
Arguments:
- echoes: bfloat16 [64, 2, 2, 16384], P(('pulse', 'tile')), may hold values from -6 to 6
- pulse_slope: bfloat16 [64, 2], P(('pulse', 'tile')), may hold values from -0.023925781 to 0.023925781
- pulse_shift: bfloat16 [64, 2], P(('pulse', 'tile')), may hold values from -3.140625 to 3.140625
- footprint: int32 [4, 8, 8], P('pulse'), may hold values from -1 to 15, as said below
- band_start: int32 [256], P('tile'), may hold values from 0 to 13216
- row_phase: float32 [256], P('tile'), may hold values from -1 to 1
Outputs:
- formed_image: float32 [2, 256, 4096], P(None, 'tile', 'pulse')
The draws below stay inside these ranges and needn't reach their ends.
Inputs may be any that keep to these rules, and one draw needn't show every extreme that they name: footprint[g, t] lists in rising order the numbers of group g's blocks whose echoes reach row strip t, then -1 to the end. It names at most one block of each run of 2 numbers that starts at a multiple of 2. In every group some list has 8 entries.
All inputs are finite; a program needn't handle non-finite values.
Results may differ from the reference program's by a relative error of at most 0.0039.
Values may be sent and summed in bfloat16 or wider, within the bound.
A program may use at most 64 MiB of HBM per device.

```python
import jax
import jax.numpy as jnp
from jax import lax

R = 16384
NCOL = 4096
TR = 32
PB = 2
BLK_DEV = 2
ITERS = 2
GROUPS = 4
STRIPS = 8
WINDOW = 3168
GROUP_BLOCKS = 16
NBLOCKS = 64
NROW = 256
LIST = 8


def draw_footprint(key, part):
    pick_key = jax.random.fold_in(key, 11)
    heavy_key = jax.random.fold_in(key, 12)
    member_key = jax.random.fold_in(key, 13)
    picked = jax.random.randint(pick_key, (GROUPS, STRIPS, STRIPS), 0, 10) < 4
    heavy_strip = jax.random.randint(heavy_key, (GROUPS,), 0, STRIPS)
    strip_ids = jnp.arange(STRIPS, dtype=jnp.int32)
    is_heavy = strip_ids[None, :, None] == heavy_strip[:, None, None]
    picked = picked | is_heavy
    member = jax.random.randint(member_key, (GROUPS, STRIPS, STRIPS), 0, BLK_DEV)
    last_source = strip_ids[None, None, :] == STRIPS - 1
    member = jnp.where(is_heavy & last_source, BLK_DEV - 1, member)
    block_ids = strip_ids[None, None, :] * BLK_DEV + member
    sort_keys = jnp.where(picked, block_ids, BLK_DEV * STRIPS + block_ids)
    ordering = jnp.argsort(sort_keys, axis=-1)
    sorted_ids = jnp.take_along_axis(block_ids, ordering, axis=-1)
    sorted_used = jnp.take_along_axis(picked, ordering, axis=-1)
    return jnp.where(sorted_used, sorted_ids, -1).astype(jnp.int32)


def touch_ends(result, key, low, largest):
    extent = result.shape
    place = [jax.random.randint(jax.random.fold_in(key, axis), (), 0, extent[axis]) for axis in range(len(extent))]
    result = result.at[tuple(place)].set(low)
    longest = extent.index(max(extent))
    place[longest] = (place[longest] + 1) % extent[longest]
    return result.at[tuple(place)].set(largest)


def levels(rng, shape, pieces, low, top_value):
    factor_of = 1.0
    for axis_at, parts in pieces:
        heights = jax.random.uniform(jax.random.fold_in(jax.random.fold_in(rng, 6), axis_at), (parts,), jnp.float32, low / len(pieces), top_value / len(pieces))
        factor_of = factor_of * jnp.repeat(jnp.exp(heights), shape[axis_at] // parts).reshape((-1,) + (1,) * (len(shape) - 1 - axis_at))
    return factor_of


def bell_draw(own_key, shape, deviation, reach, split=(), kind=jnp.bfloat16):
    result = deviation * jax.random.normal(own_key, shape, jnp.float32)
    if split:
        result = result * levels(own_key, shape, split, -0.22, 0.18)
    return jnp.clip(result, -reach, reach).astype(kind)


def setup_inputs(seed: int = 0) -> dict:
    streams_of = jax.random.split(jax.random.key(seed), 7)
    return {
        "echoes": bell_draw(streams_of[0], (NBLOCKS, PB, 2, R), 1.0, 6.0, ((0, 32),)),
        "pulse_slope": jnp.clip(jax.random.uniform(streams_of[1], (NBLOCKS, PB), jnp.float32, -0.023925781, 0.023925781) * levels(streams_of[1], (NBLOCKS, PB), ((0, 32),), -0.4, 0.0), -0.023925781, 0.023925781).astype(jnp.bfloat16),
        "pulse_shift": jnp.clip(jax.random.uniform(streams_of[2], (NBLOCKS, PB), jnp.float32, -3.140625, 3.140625), -3.140625, 3.140625).astype(jnp.bfloat16),
        "footprint": draw_footprint(jax.random.fold_in(streams_of[6], 71), 0),
        "band_start": touch_ends(jax.random.randint(streams_of[4], (NROW,), 0, R - WINDOW + 1), jax.random.fold_in(streams_of[4], 1), 0, R - WINDOW).astype(jnp.int32),
        "row_phase": jnp.clip(jax.random.uniform(streams_of[5], (NROW,), jnp.float32, -1.0, 1.0) * levels(streams_of[5], (NROW,), ((0, 8),), -0.4, 0.0), -1.0, 1.0),
    }


step_size = 0.5
tv_weight = 0.4
floor_square = 0.25

def cubic_table():
    columns = jnp.arange(128, dtype=jnp.int32)
    quarter_pos = 3 * columns + 4
    base_tap = quarter_pos // 4
    fraction = (quarter_pos % 4).astype(jnp.float32) / 4.0
    fraction_sq = fraction * fraction
    fraction_cube = fraction_sq * fraction
    weights = [(-fraction_cube + 2.0 * fraction_sq - fraction) * 0.5, (3.0 * fraction_cube - 5.0 * fraction_sq + 2.0) * 0.5, (-3.0 * fraction_cube + 4.0 * fraction_sq + fraction) * 0.5, (fraction_cube - fraction_sq) * 0.5]
    tap_rows = jnp.arange(128, dtype=jnp.int32)[:, None]
    cubic_weights = jnp.zeros((128, 128), jnp.float32)
    for tap_shift, weight in zip(range(-1, 3), weights):
        cubic_weights = cubic_weights + jnp.where(tap_rows == (base_tap + tap_shift)[None, :], weight[None, :], 0.0)
    return cubic_weights

def block_image(block_echo, block_slope, block_shift, band_start, row_phase, cubic_weights):
    pulses = block_echo.shape[0]
    row_count = band_start.shape[0]
    col_blocks = NCOL // 128
    window_span = 96 * (col_blocks + 1)
    flat_echo = block_echo.reshape(pulses * 2, block_echo.shape[2])
    segments = jax.vmap(lambda row_start: lax.dynamic_slice_in_dim(flat_echo, row_start, window_span, axis=1))(band_start)
    leading = segments[..., :96 * col_blocks].reshape(row_count, pulses * 2, col_blocks, 96)
    trailing = segments[..., 96:].reshape(row_count, pulses * 2, col_blocks, 96)[..., :32]
    windows = jnp.concatenate([leading, trailing], axis=-1)
    windows = jnp.transpose(windows, (0, 2, 1, 3)).reshape(row_count, col_blocks, pulses, 2, 128).astype(jnp.float32)
    slopes = block_slope.astype(jnp.float32)
    shifts = block_shift.astype(jnp.float32)
    block_pos = (128 * jnp.arange(col_blocks, dtype=jnp.int32)).astype(jnp.float32)
    angle_grid = shifts[None, None, :] * row_phase[:, None, None] + slopes[None, None, :] * block_pos[None, :, None]
    cosine = jnp.cos(angle_grid)[..., None]
    sines = jnp.sin(angle_grid)[..., None]
    real_part = windows[:, :, :, 0]
    imag_part = windows[:, :, :, 1]
    turned_re = real_part * cosine - imag_part * sines
    turned_im = real_part * sines + imag_part * cosine
    turned = jnp.stack([turned_re, turned_im], axis=3).astype(jnp.bfloat16).reshape(row_count * col_blocks, pulses * 256)
    column_pos = jnp.arange(128, dtype=jnp.int32).astype(jnp.float32)
    column_ramp = slopes[:, None] * column_pos[None, :]
    kernel_re = cubic_weights[None] * jnp.cos(column_ramp)[:, None, :]
    kernel_im = cubic_weights[None] * jnp.sin(column_ramp)[:, None, :]
    upper_rows = jnp.concatenate([kernel_re, kernel_im], axis=2)
    bottom = jnp.concatenate([-kernel_im, kernel_re], axis=2)
    kernel = jnp.stack([upper_rows, bottom], axis=1).astype(jnp.bfloat16).reshape(pulses * 256, 256)
    product = jnp.dot(turned, kernel, preferred_element_type=jnp.float32)
    return product.reshape(row_count, col_blocks, 256)

def tv_update(field, padded, base_image, row_anchor, col_anchor, grid_rows, grid_cols):
    row_count = field.shape[1]
    col_count = field.shape[2]
    grad_rows = padded[:, 1:row_count + 2, 0:col_count + 1] - padded[:, 0:row_count + 1, 0:col_count + 1]
    grad_cols = padded[:, 0:row_count + 1, 1:col_count + 2] - padded[:, 0:row_count + 1, 0:col_count + 1]
    row_ids = row_anchor - 1 + jnp.arange(row_count + 1, dtype=jnp.int32)
    col_ids = col_anchor - 1 + jnp.arange(col_count + 1, dtype=jnp.int32)
    inside = (row_ids >= 0)[:, None] & (col_ids >= 0)[None, :]
    grad_rows = jnp.where((inside & (row_ids < grid_rows - 1)[:, None])[None], grad_rows, 0.0)
    grad_cols = jnp.where((inside & (col_ids < grid_cols - 1)[None, :])[None], grad_cols, 0.0)
    magnitude = jnp.sqrt(lax.optimization_barrier(jnp.sum(grad_rows * grad_rows + grad_cols * grad_cols, axis=0)) + floor_square)
    flux_rows = grad_rows / magnitude[None]
    flux_cols = grad_cols / magnitude[None]
    divergence = flux_rows[:, 1:, 1:] - flux_rows[:, :-1, 1:] + flux_cols[:, 1:, 1:] - flux_cols[:, 1:, :-1]
    return field - step_size * (field - base_image - tv_weight * divergence)

def reference(echoes, pulse_slope, pulse_shift, footprint, band_start, row_phase):
    cubic_weights = cubic_table()
    col_blocks = NCOL // 128

    def strip_image(strip_index):
        starts = lax.dynamic_slice_in_dim(band_start, strip_index * TR, TR)
        phases = lax.dynamic_slice_in_dim(row_phase, strip_index * TR, TR)
        entries = lax.dynamic_index_in_dim(footprint, strip_index, axis=1, keepdims=False).reshape(-1)
        group_ids = jnp.repeat(jnp.arange(GROUPS, dtype=jnp.int32), LIST)

        def add_block(running, list_entry):
            group_index, block_id = list_entry

            def used_branch(partial_sum):
                global_id = (group_index * GROUP_BLOCKS + block_id).astype(jnp.int32)
                block_echo = lax.dynamic_index_in_dim(echoes, global_id, 0, keepdims=False)
                block_slope = lax.dynamic_index_in_dim(pulse_slope, global_id, 0, keepdims=False)
                block_shift = lax.dynamic_index_in_dim(pulse_shift, global_id, 0, keepdims=False)
                return partial_sum + block_image(block_echo, block_slope, block_shift, starts, phases, cubic_weights)
            return (lax.cond(block_id >= 0, used_branch, lambda partial_sum: partial_sum, running), None)
        zero_image = jnp.zeros((TR, col_blocks, 256), jnp.float32)
        running, _ = lax.scan(add_block, zero_image, (group_ids, entries))
        return running
    strips_out = lax.map(strip_image, jnp.arange(STRIPS, dtype=jnp.int32))
    real_plane = strips_out[..., :128].reshape(NROW, NCOL)
    imag_plane = strips_out[..., 128:].reshape(NROW, NCOL)
    normalize = (PB * STRIPS * GROUPS) ** (-0.5)
    base_image = jnp.stack([real_plane, imag_plane]) * normalize
    field = base_image
    for iteration in range(ITERS):
        padded = jnp.pad(field, ((0, 0), (1, 1), (1, 1)))
        field = tv_update(field, padded, base_image, 0, 0, NROW, NCOL)
    return field
```

```python
import functools

import jax
import jax.numpy as jnp
import numpy as np
from jax import lax
from jax.experimental import pallas as pl
from jax.experimental.pallas import tpu as pltpu
from jax.sharding import PartitionSpec as P

NCOL = 4096
ITERS = 2
KBLOCKS = NCOL // 128
QUADS = KBLOCKS // 4
HALO = ITERS

step_size = 0.5
tv_weight = 0.4
floor_square = 0.25

MESH = pl.DeviceIdType.MESH
F32 = jnp.float32
BF16 = jnp.bfloat16


def interpolation_table():
    columns = np.arange(128)
    position = 3 * columns + 4
    base = position // 4
    f = (position % 4) / 4.0
    weights = [
        (-(f**3) + 2 * f**2 - f) / 2,
        (3 * f**3 - 5 * f**2 + 2) / 2,
        (-3 * f**3 + 4 * f**2 + f) / 2,
        (f**3 - f**2) / 2,
    ]
    table = np.zeros((512, 512), np.float32)
    for q in range(4):
        for shift, weight in zip(range(-1, 3), weights):
            table[96 * q + base + shift, 128 * q + columns] += weight
    return table


def exchange_kernel(n, blocks_ref, params_ref, got_ref, got_params_ref, sends, recvs, local_sem):
    me = lax.axis_index("tile")
    barrier = pltpu.get_barrier_semaphore()
    for d in range(1, n):
        pl.semaphore_signal(
            barrier, inc=1, device_id={"tile": lax.rem(me + d, n)}, device_id_type=MESH
        )
    own = pltpu.make_async_copy(blocks_ref.at[me], got_ref.at[me], local_sem.at[0])
    own_params = pltpu.make_async_copy(params_ref.at[me], got_params_ref.at[me], local_sem.at[1])
    own.start()
    own_params.start()
    pl.semaphore_wait(barrier, n - 1)
    copies = []
    for d in range(1, n):
        target = lax.rem(me + d, n)
        for j, (src, dst) in enumerate(((params_ref, got_params_ref), (blocks_ref, got_ref))):
            copy = pltpu.make_async_remote_copy(
                src_ref=src.at[target],
                dst_ref=dst.at[me],
                send_sem=sends.at[j, d],
                recv_sem=recvs.at[j, d],
                device_id={"tile": target},
                device_id_type=MESH,
            )
            copy.start()
            copies.append(copy)
    own.wait()
    own_params.wait()
    for copy in copies:
        copy.wait()


def exchange(blocks, params):
    n = blocks.shape[0]
    return pl.pallas_call(
        functools.partial(exchange_kernel, n),
        out_shape=(
            jax.ShapeDtypeStruct(blocks.shape, blocks.dtype),
            jax.ShapeDtypeStruct(params.shape, params.dtype),
        ),
        in_specs=[pl.BlockSpec(memory_space=pl.ANY)] * 2,
        out_specs=[pl.BlockSpec(memory_space=pl.ANY)] * 2,
        scratch_shapes=[
            pltpu.SemaphoreType.DMA((2, n)),
            pltpu.SemaphoreType.DMA((2, n)),
            pltpu.SemaphoreType.DMA((2,)),
        ],
        compiler_params=pltpu.CompilerParams(collective_id=0, has_side_effects=True),
    )(blocks, params)


def image_kernel(
    pulses,
    groups,
    used_ref,
    start_ref,
    echo_ref,
    params_ref,
    phase_ref,
    table_ref,
    out_ref,
    wide,
    turned,
    lhs,
    product,
    ramp,
    rowturn,
    acc,
    image,
):
    n = echo_ref.shape[0]
    bins = echo_ref.shape[2]
    rows = phase_ref.shape[0]
    share = KBLOCKS // groups
    scale = float(pulses * n * groups) ** -0.5
    lane = lax.broadcasted_iota(jnp.int32, (8, 128), 1)
    sub = lax.broadcasted_iota(jnp.int32, (8, 128), 0)
    wide[:, bins:, :] = jnp.zeros((2 * pulses, wide.shape[1] - bins, 128), F32)
    acc[...] = jnp.zeros_like(acc)

    def slot(s, carry):
        @pl.when(used_ref[s] > 0)
        def _():
            wide[:, :bins, :] = echo_ref[s].astype(F32)
            for p in range(pulses):
                slope = params_ref[s, p : p + 1, :]
                shift = params_ref[s, pulses + p : pulses + p + 1, :]
                turn = phase_ref[...] * shift
                rowturn[p, 0] = jnp.cos(turn)
                rowturn[p, 1] = jnp.sin(turn)
                for q in range(4):
                    angle = (512 * sub + 128 * q + lane).astype(F32) * slope
                    ramp[p, 0, q] = jnp.cos(angle)
                    ramp[p, 1, q] = jnp.sin(angle)

            def gather(pair, c):
                for plane in range(2 * pulses):
                    halves = []
                    for h in range(2):
                        begin = start_ref[2 * pair + h]
                        tile = begin // 128
                        off = begin - 128 * tile
                        spot = 2 * plane + h
                        turned[spot] = pltpu.roll(
                            wide[plane, pl.ds(tile, 32), :], lax.rem(128 - off, 128), 1
                        )
                        ys = [turned[spot, pl.ds(o, 8, stride=3), :] for o in range(5)]
                        first = lane < 128 - off
                        halves.append(
                            [jnp.where(first, ys[j], ys[j + 1]) for j in range(4)]
                        )
                    for j in range(4):
                        both = jnp.concatenate([halves[0][j], halves[1][j]], axis=0)
                        lhs[plane, pl.ds(pl.multiple_of(16 * pair, 16), 16), 128 * j : 128 * j + 128] = both.astype(BF16)
                return c

            lax.fori_loop(0, rows // 2, gather, 0)
            for plane in range(2 * pulses):
                product[plane, :, 0:256] = jnp.dot(
                    lhs[plane, :, 0:256], table_ref[0:256, 0:256], preferred_element_type=F32
                )
                product[plane, :, 256:512] = jnp.dot(
                    lhs[plane], table_ref[:, 256:512], preferred_element_type=F32
                )

            def turn_row(r, c):
                at = pl.ds(pl.multiple_of(8 * r, 8), 8)
                for q in range(4):
                    total_re = acc[0, r, q]
                    total_im = acc[1, r, q]
                    for p in range(pulses):
                        row_re = rowturn[p, 0, pl.ds(r, 1), :]
                        row_im = rowturn[p, 1, pl.ds(r, 1), :]
                        ramp_re = ramp[p, 0, q]
                        ramp_im = ramp[p, 1, q]
                        re = ramp_re * row_re - ramp_im * row_im
                        im = ramp_re * row_im + ramp_im * row_re
                        value_re = product[2 * p, at, 128 * q : 128 * q + 128]
                        value_im = product[2 * p + 1, at, 128 * q : 128 * q + 128]
                        total_re = total_re + (value_re * re - value_im * im)
                        total_im = total_im + (value_re * im + value_im * re)
                    acc[0, r, q] = total_re
                    acc[1, r, q] = total_im
                return c

            lax.fori_loop(0, rows, turn_row, 0)

        return carry

    lax.fori_loop(0, n, slot, 0)

    def place(r, c):
        for plane in range(2):
            for q in range(4):
                image[pl.ds((plane * rows + r) * KBLOCKS + q, QUADS, stride=4), :] = (
                    acc[plane, r, q] * scale
                )
        return c

    lax.fori_loop(0, rows, place, 0)

    together = 16 // share
    main = 2 * rows * share

    def emit(i, c):
        for g in range(groups):
            parts = [
                image[pl.ds((i * together + h) * KBLOCKS + share * g, share), :]
                for h in range(together)
            ]
            out_ref[g, pl.ds(pl.multiple_of(16 * i, 16), 16), :] = jnp.concatenate(
                parts, axis=0
            ).astype(BF16)
        return c

    lax.fori_loop(0, 2 * rows // together, emit, 0)
    wide_lane = lax.broadcasted_iota(jnp.int32, (rows, 128), 1)
    for g in range(groups):
        after = min(share * (g + 1), KBLOCKS - 1)
        before = max(share * g - 1, 0)
        for plane in range(2):
            edge = jnp.where(
                wide_lane < 64,
                image[pl.ds(plane * rows * KBLOCKS + after, rows, stride=KBLOCKS), :],
                image[pl.ds(plane * rows * KBLOCKS + before, rows, stride=KBLOCKS), :],
            )
            out_ref[g, main + plane * rows : main + (plane + 1) * rows, :] = edge.astype(BF16)


def partial_image(used, starts, echo, params, phases, table, pulses, groups):
    n, planes, bins, _ = echo.shape
    rows = phases.shape[0]
    share = KBLOCKS // groups
    vmem = pl.BlockSpec(memory_space=pltpu.VMEM)
    smem = pl.BlockSpec(memory_space=pltpu.SMEM)
    return pl.pallas_call(
        functools.partial(image_kernel, pulses, groups),
        out_shape=jax.ShapeDtypeStruct((groups, 2 * rows * share + 2 * rows, 128), BF16),
        in_specs=[smem, smem, vmem, vmem, vmem, vmem],
        out_specs=vmem,
        scratch_shapes=[
            pltpu.VMEM((planes, bins + 8, 128), F32),
            pltpu.VMEM((2 * planes, 32, 128), F32),
            pltpu.VMEM((planes, rows * QUADS, 512), BF16),
            pltpu.VMEM((planes, rows * QUADS, 512), F32),
            pltpu.VMEM((pulses, 2, 4, 8, 128), F32),
            pltpu.VMEM((pulses, 2, rows, 128), F32),
            pltpu.VMEM((2, rows, 4, 8, 128), F32),
            pltpu.VMEM((2 * rows * KBLOCKS, 128), F32),
        ],
        compiler_params=pltpu.CompilerParams(vmem_limit_bytes=48 * 1024 * 1024),
    )(used, starts, echo, params, phases, table)


def refine_kernel(
    rows,
    groups,
    tiles,
    part_ref,
    out_ref,
    got,
    first,
    second,
    halo,
    sends,
    recvs,
    halo_sends,
    halo_recvs,
):
    share = KBLOCKS // groups
    blocks = share + 1
    group = lax.axis_index("pulse")
    tile = lax.axis_index("tile")
    barrier = pltpu.get_barrier_semaphore()
    for d in range(1, groups):
        pl.semaphore_signal(
            barrier, inc=1, device_id={"pulse": lax.rem(group + d, groups)}, device_id_type=MESH
        )

    @pl.when(tile > 0)
    def _():
        pl.semaphore_signal(barrier, inc=1, device_id={"tile": tile - 1}, device_id_type=MESH)

    @pl.when(tile < tiles - 1)
    def _():
        pl.semaphore_signal(barrier, inc=1, device_id={"tile": tile + 1}, device_id_type=MESH)

    around = (tile > 0).astype(jnp.int32) + (tile < tiles - 1).astype(jnp.int32)
    pl.semaphore_wait(barrier, groups - 1 + around)

    copies = []
    for d in range(1, groups):
        target = lax.rem(group + d, groups)
        copy = pltpu.make_async_remote_copy(
            src_ref=part_ref.at[target],
            dst_ref=got.at[d - 1],
            send_sem=sends.at[d - 1],
            recv_sem=recvs.at[d - 1],
            device_id={"pulse": target},
            device_id_type=MESH,
        )
        copy.start()
        copies.append(copy)
    for copy in copies:
        copy.wait()

    main = 2 * rows * share
    total = part_ref[group].astype(F32)
    for d in range(1, groups):
        total = total + got[d - 1].astype(F32)
    for plane in range(2):
        first[plane, HALO : HALO + rows, 0:share, :] = total[
            plane * rows * share : (plane + 1) * rows * share
        ].reshape(rows, share, 128)
        for r in range(rows):
            at = main + plane * rows + r
            first[plane, HALO + r, share:blocks, :] = total[at : at + 1]

    def upward():
        return pltpu.make_async_remote_copy(
            src_ref=first.at[:, pl.ds(HALO, HALO)],
            dst_ref=halo.at[1],
            send_sem=halo_sends.at[1],
            recv_sem=halo_recvs.at[1],
            device_id={"tile": tile - 1},
            device_id_type=MESH,
        )

    def downward():
        return pltpu.make_async_remote_copy(
            src_ref=first.at[:, pl.ds(rows, HALO)],
            dst_ref=halo.at[0],
            send_sem=halo_sends.at[0],
            recv_sem=halo_recvs.at[0],
            device_id={"tile": tile + 1},
            device_id_type=MESH,
        )

    @pl.when(tile > 0)
    def _():
        upward().start()

    @pl.when(tile < tiles - 1)
    def _():
        downward().start()

    @pl.when(tile > 0)
    def _():
        downward().wait_recv()
        first[:, 0:HALO] = halo[0]

    @pl.when(tile == 0)
    def _():
        first[:, 0:HALO] = jnp.zeros_like(first[:, 0:HALO])

    @pl.when(tile < tiles - 1)
    def _():
        upward().wait_recv()
        first[:, HALO + rows :] = halo[1]

    @pl.when(tile == tiles - 1)
    def _():
        first[:, HALO + rows :] = jnp.zeros_like(first[:, 0:HALO])

    @pl.when(tile > 0)
    def _():
        upward().wait_send()

    @pl.when(tile < tiles - 1)
    def _():
        downward().wait_send()

    shape = (2, blocks, 128)
    lane = lax.broadcasted_iota(jnp.int32, shape, 2)
    block = lax.broadcasted_iota(jnp.int32, shape, 1)
    column = group * share * 128 + block * 128 + lane
    edge_column = jnp.where(lane < 64, column, group * share * 128 + lane - 128)
    column = jnp.where(block == share, edge_column, column)
    column_in = (column >= 0) & (column < NCOL)
    has_right = (column >= 0) & (column < NCOL - 1)
    keep_row = jnp.where(column_in, 1.0, 0.0).astype(F32)
    keep_col = jnp.where(has_right, 1.0, 0.0).astype(F32)
    row_base = tile * rows - HALO
    grid_rows = tiles * rows

    def right_of(x):
        following = jnp.concatenate([x[:, 1:], x[:, :1]], axis=1)
        return jnp.where(lane == 127, pltpu.roll(following, 127, 2), pltpu.roll(x, 127, 2))

    def left_of(x):
        preceding = jnp.concatenate([x[:, share:], x[:, :share]], axis=1)
        return jnp.where(lane == 0, pltpu.roll(preceding, 1, 2), pltpu.roll(x, 1, 2))

    def flux(source, i):
        here = source[:, i, 0:blocks, :]
        row = row_base + i
        row_in = ((row >= 0) & (row < grid_rows)).astype(F32)
        below_in = ((row >= 0) & (row < grid_rows - 1)).astype(F32)
        down = (source[:, i + 1, 0:blocks, :] - here) * (keep_row * below_in)
        right = (right_of(here) - here) * (keep_col * row_in)
        square = jnp.sum(down * down + right * right, axis=0, keepdims=True) + floor_square
        inverse = lax.rsqrt(square)
        return here, down * inverse, right * inverse

    def sweep(source, low, high, write):
        _, above, _ = flux(source, low - 1)

        def one(i, above):
            here, down, right = flux(source, i)
            divergence = down - above + right - left_of(right)
            base = first[:, i, 0:blocks, :]
            write(i, here - step_size * (here - base - tv_weight * divergence))
            return down

        lax.fori_loop(low, high, one, above, unroll=2)

    def write_second(i, value):
        second[:, i, 0:blocks, :] = value

    def write_out(i, value):
        out_ref[:, i - HALO] = value[:, 0:share]

    sweep(first, 1, rows + 2 * HALO - 1, write_second)
    sweep(second, 2, rows + 2 * HALO - 2, write_out)


def refine(partial, rows, groups, tiles):
    share = KBLOCKS // groups
    padded = -(-(share + 1) // 8) * 8
    extent = rows + 2 * HALO
    return pl.pallas_call(
        functools.partial(refine_kernel, rows, groups, tiles),
        out_shape=jax.ShapeDtypeStruct((2, rows, share, 128), F32),
        in_specs=[pl.BlockSpec(memory_space=pltpu.VMEM)],
        out_specs=pl.BlockSpec(memory_space=pltpu.VMEM),
        scratch_shapes=[
            pltpu.VMEM((groups - 1,) + partial.shape[1:], BF16),
            pltpu.VMEM((2, extent, padded, 128), F32),
            pltpu.VMEM((2, extent, padded, 128), F32),
            pltpu.VMEM((2, 2, HALO, padded, 128), F32),
            pltpu.SemaphoreType.DMA((groups - 1,)),
            pltpu.SemaphoreType.DMA((groups - 1,)),
            pltpu.SemaphoreType.DMA((2,)),
            pltpu.SemaphoreType.DMA((2,)),
        ],
        compiler_params=pltpu.CompilerParams(
            collective_id=1, has_side_effects=True, vmem_limit_bytes=48 * 1024 * 1024
        ),
    )(partial)


def body(echoes, pulse_slope, pulse_shift, footprint, band_start, row_phase):
    tiles = lax.axis_size("tile")
    groups = lax.axis_size("pulse")
    tile = lax.axis_index("tile")
    held, pulses = pulse_slope.shape
    rows = band_start.shape[0]
    bins = echoes.shape[3] // 128
    lists = footprint[0]
    wanted = [jnp.any(lists == tile * held + b, axis=1) for b in range(held)]
    planes = echoes.reshape(held, pulses * 2, bins, 128)
    params = jnp.concatenate([pulse_slope, pulse_shift], axis=1).astype(F32)
    params = jnp.pad(params, ((0, 0), (0, -(2 * pulses) % 8)))
    blocks = jnp.broadcast_to(planes[0][None], (tiles,) + planes.shape[1:])
    values = jnp.broadcast_to(params[0][None], (tiles, params.shape[1]))
    for b in range(1, held):
        blocks = jnp.where(wanted[b][:, None, None, None], planes[b][None], blocks)
        values = jnp.where(wanted[b][:, None], params[b][None], values)
    values = jnp.broadcast_to(values[:, :, None], values.shape + (128,))
    got, got_params = exchange(blocks, values)

    own_list = lax.dynamic_index_in_dim(lists, tile, axis=0, keepdims=False)
    sources = jnp.arange(tiles, dtype=jnp.int32)
    used = jnp.any(
        (own_list[None, :] >= 0) & (own_list[None, :] // held == sources[:, None]), axis=1
    ).astype(jnp.int32)
    phases = jnp.broadcast_to(row_phase[:, None], (rows, 128))
    table = jnp.asarray(interpolation_table(), BF16)
    partial = partial_image(used, band_start, got, got_params, phases, table, pulses, groups)
    refined = refine(partial, rows, groups, tiles)
    return refined.reshape(2, rows, NCOL // groups)


def solution(mesh):
    in_specs = (
        P(("pulse", "tile"), None, None, None),
        P(("pulse", "tile"), None),
        P(("pulse", "tile"), None),
        P("pulse", None, None),
        P("tile"),
        P("tile"),
    )
    out_specs = P(None, "tile", "pulse")
    return jax.shard_map(body, mesh=mesh, in_specs=in_specs, out_specs=out_specs, check_vma=False)
```

```python
import functools

import jax
import jax.numpy as jnp
import numpy as np
from jax import lax
from jax.experimental import pallas as pl
from jax.experimental.pallas import tpu as pltpu
from jax.sharding import PartitionSpec as P

NCOL = 4096
ITERS = 2
KBLOCKS = NCOL // 128
QUADS = KBLOCKS // 4
HALO = ITERS

step_size = 0.5
tv_weight = 0.4
floor_square = 0.25

MESH = pl.DeviceIdType.MESH
F32 = jnp.float32
BF16 = jnp.bfloat16


def interpolation_table():
    columns = np.arange(128)
    position = 3 * columns + 4
    base = position // 4
    f = (position % 4) / 4.0
    weights = [
        (-(f**3) + 2 * f**2 - f) / 2,
        (3 * f**3 - 5 * f**2 + 2) / 2,
        (-3 * f**3 + 4 * f**2 + f) / 2,
        (f**3 - f**2) / 2,
    ]
    table = np.zeros((512, 512), np.float32)
    for q in range(4):
        for shift, weight in zip(range(-1, 3), weights):
            table[96 * q + base + shift, 128 * q + columns] += weight
    return table


def sine_cosine(angle):
    turns = jnp.floor(angle * 0.6366197723675814 + 0.5)
    rest = angle - turns * 1.5703125
    rest = rest - turns * 4.837512969970703125e-4
    rest = rest - turns * 7.549789948768648e-8
    square = rest * rest
    sine = rest + rest * square * (
        -1.6666654611e-1 + square * (8.3321608736e-3 - square * 1.9515295891e-4)
    )
    cosine = (1.0 - 0.5 * square) + square * square * (
        4.166664568298827e-2 + square * (-1.388731625493765e-3 + square * 2.443315711809948e-5)
    )
    quarter = turns - 4.0 * jnp.floor(turns * 0.25)
    odd = (quarter == 1.0) | (quarter == 3.0)
    sine_sign = jnp.where(quarter >= 2.0, -1.0, 1.0)
    cosine_sign = jnp.where((quarter == 1.0) | (quarter == 2.0), -1.0, 1.0)
    return (
        sine_sign * jnp.where(odd, cosine, sine),
        cosine_sign * jnp.where(odd, sine, cosine),
    )


def kernel(
    held,
    pulses,
    rows,
    groups,
    n,
    lists_ref,
    start_ref,
    echo_ref,
    phase_ref,
    table_ref,
    out_ref,
    picked,
    got,
    wide,
    turned,
    lhs,
    product,
    ramp,
    rowturn,
    acc,
    image,
    part,
    got_part,
    first,
    second,
    halo,
    sends,
    recvs,
    part_sends,
    part_recvs,
    halo_sends,
    halo_recvs,
):
    bins = (echo_ref.shape[1] - 16) // (2 * pulses)
    planes = 2 * pulses
    share = KBLOCKS // groups
    blocks = share + 1
    scale = float(pulses * n * groups) ** -0.5
    group = lax.axis_index("pulse")
    tile = lax.axis_index("tile")
    power = n & (n - 1) == 0

    def partner(d):
        if not power:
            return lax.rem(n + d - tile, n)
        other = tile
        bit = 1
        while bit < n:
            other = other + ((d // bit) % 2) * bit * (1 - 2 * ((tile // bit) % 2))
            bit *= 2
        return other

    barrier = pltpu.get_barrier_semaphore()
    for d in range(1, groups):
        pl.semaphore_signal(
            barrier, inc=1, device_id={"pulse": lax.rem(group + d, groups)}, device_id_type=MESH
        )
    for d in range(1, n):
        pl.semaphore_signal(
            barrier, inc=1, device_id={"tile": lax.rem(tile + d, n)}, device_id_type=MESH
        )

    def names(strip, number):
        found = lists_ref[strip, 0] == number
        for j in range(1, lists_ref.shape[1]):
            found = found | (lists_ref[strip, j] == number)
        return found

    def pick(d, c):
        other = partner(d)
        block = echo_ref[0]
        for b in range(1, held):
            block = jnp.where(names(other, tile * held + b), echo_ref[b], block)
        picked[d] = block
        return c

    lax.fori_loop(0, n, pick, 0)
    pl.semaphore_wait(barrier, n - 1 + groups - 1)

    def block_copy(d):
        return pltpu.make_async_remote_copy(
            src_ref=picked.at[d],
            dst_ref=got.at[d],
            send_sem=sends.at[d],
            recv_sem=recvs.at[d],
            device_id={"tile": partner(d)},
            device_id_type=MESH,
        )

    def send(i, c):
        block_copy(n - i).start()
        return c

    lax.fori_loop(1, n, send, 0)

    lane = lax.broadcasted_iota(jnp.int32, (8, 128), 1)
    sub = lax.broadcasted_iota(jnp.int32, (8, 128), 0)
    wide[:, bins:, :] = jnp.zeros((planes, wide.shape[1] - bins, 128), F32)
    acc[...] = jnp.zeros_like(acc)
    column_in_quad = (512 * sub + lane).astype(F32)

    def compute(d, block):
        source = partner(d)
        used = names(tile, source * held)
        for b in range(1, held):
            used = used | names(tile, source * held + b)
        weight = jnp.where(used, 1.0, 0.0).astype(F32)
        wide[:, :bins, :] = block[: planes * bins].astype(F32).reshape(planes, bins, 128)
        tail = block[planes * bins :].astype(F32)
        for p in range(pulses):
            slope = tail[p : p + 1]
            shift = tail[pulses + p : pulses + p + 1]
            turn_im, turn_re = sine_cosine(phase_ref[...] * shift)
            rowturn[p, 0] = turn_re
            rowturn[p, 1] = turn_im
            im, re = sine_cosine(column_in_quad * slope)
            step_im, step_re = sine_cosine(jnp.broadcast_to(128.0 * slope, (8, 128)))
            re = re * weight
            im = im * weight
            for q in range(4):
                ramp[p, 0, q] = re
                ramp[p, 1, q] = im
                re, im = re * step_re - im * step_im, re * step_im + im * step_re

        def gather(pair, c):
            for plane in range(planes):
                halves = []
                for h in range(2):
                    begin = start_ref[2 * pair + h]
                    at = begin // 128
                    off = begin - 128 * at
                    spot = 2 * plane + h
                    turned[spot] = pltpu.roll(
                        wide[plane, pl.ds(at, 32), :], lax.rem(128 - off, 128), 1
                    )
                    ys = [turned[spot, pl.ds(o, 8, stride=3), :] for o in range(5)]
                    keep = lane < 128 - off
                    halves.append([jnp.where(keep, ys[j], ys[j + 1]) for j in range(4)])
                for j in range(4):
                    both = jnp.concatenate([halves[0][j], halves[1][j]], axis=0)
                    lhs[
                        plane, pl.ds(pl.multiple_of(16 * pair, 16), 16), 128 * j : 128 * j + 128
                    ] = both.astype(BF16)
            return c

        lax.fori_loop(0, rows // 2, gather, 0, unroll=2)
        for plane in range(planes):
            product[plane, :, 0:256] = jnp.dot(
                lhs[plane, :, 0:256], table_ref[0:256, 0:256], preferred_element_type=F32
            )
            product[plane, :, 256:512] = jnp.dot(
                lhs[plane], table_ref[:, 256:512], preferred_element_type=F32
            )

        def turn_row(r, c):
            at = pl.ds(pl.multiple_of(8 * r, 8), 8)
            for q in range(4):
                total_re = acc[0, r, q]
                total_im = acc[1, r, q]
                for p in range(pulses):
                    row_re = rowturn[p, 0, pl.ds(r, 1), :]
                    row_im = rowturn[p, 1, pl.ds(r, 1), :]
                    ramp_re = ramp[p, 0, q]
                    ramp_im = ramp[p, 1, q]
                    re = ramp_re * row_re - ramp_im * row_im
                    im = ramp_re * row_im + ramp_im * row_re
                    value_re = product[2 * p, at, 128 * q : 128 * q + 128]
                    value_im = product[2 * p + 1, at, 128 * q : 128 * q + 128]
                    total_re = total_re + (value_re * re - value_im * im)
                    total_im = total_im + (value_re * im + value_im * re)
                acc[0, r, q] = total_re
                acc[1, r, q] = total_im
            return c

        lax.fori_loop(0, rows, turn_row, 0, unroll=2)

    def slot(d, c):
        block_copy(d).wait_recv()
        compute(d, got[d])
        return c

    compute(0, picked[0])
    lax.fori_loop(1, n, slot, 0)

    def sent(d, c):
        block_copy(d).wait_send()
        return c

    lax.fori_loop(1, n, sent, 0)

    def place(r, c):
        for plane in range(2):
            for q in range(4):
                image[pl.ds((plane * rows + r) * KBLOCKS + q, QUADS, stride=4), :] = (
                    acc[plane, r, q] * scale
                )
        return c

    lax.fori_loop(0, rows, place, 0, unroll=2)

    together = 16 // share
    main = 2 * rows * share
    wide_lane = lax.broadcasted_iota(jnp.int32, (rows, 128), 1)

    def emit_for(g):
        def emit(i, c):
            parts = [
                image[pl.ds((i * together + h) * KBLOCKS + share * g, share), :]
                for h in range(together)
            ]
            part[g, pl.ds(pl.multiple_of(16 * i, 16), 16), :] = jnp.concatenate(
                parts, axis=0
            ).astype(BF16)
            return c

        lax.fori_loop(0, 2 * rows // together, emit, 0, unroll=4)
        after = jnp.minimum(share * (g + 1), KBLOCKS - 1)
        before = jnp.maximum(share * g - 1, 0)
        for plane in range(2):
            edge = jnp.where(
                wide_lane < 64,
                image[pl.ds(plane * rows * KBLOCKS + after, rows, stride=KBLOCKS), :],
                image[pl.ds(plane * rows * KBLOCKS + before, rows, stride=KBLOCKS), :],
            )
            part[g, main + plane * rows : main + (plane + 1) * rows, :] = edge.astype(BF16)

    copies = []
    for d in range(groups - 1, 0, -1):
        target = lax.rem(group + d, groups)
        emit_for(target)
        copy = pltpu.make_async_remote_copy(
            src_ref=part.at[target],
            dst_ref=got_part.at[d - 1],
            send_sem=part_sends.at[d - 1],
            recv_sem=part_recvs.at[d - 1],
            device_id={"pulse": target},
            device_id_type=MESH,
        )
        copy.start()
        copies.append(copy)
    emit_for(group)
    for copy in copies:
        copy.wait()

    total = part[group].astype(F32)
    for d in range(1, groups):
        total = total + got_part[d - 1].astype(F32)
    for plane in range(2):
        first[plane, HALO : HALO + rows, 0:share, :] = total[
            plane * rows * share : (plane + 1) * rows * share
        ].reshape(rows, share, 128)
        for r in range(rows):
            at = main + plane * rows + r
            first[plane, HALO + r, share:blocks, :] = total[at : at + 1]

    def upward():
        return pltpu.make_async_remote_copy(
            src_ref=first.at[:, pl.ds(HALO, HALO)],
            dst_ref=halo.at[1],
            send_sem=halo_sends.at[1],
            recv_sem=halo_recvs.at[1],
            device_id={"tile": tile - 1},
            device_id_type=MESH,
        )

    def downward():
        return pltpu.make_async_remote_copy(
            src_ref=first.at[:, pl.ds(rows, HALO)],
            dst_ref=halo.at[0],
            send_sem=halo_sends.at[0],
            recv_sem=halo_recvs.at[0],
            device_id={"tile": tile + 1},
            device_id_type=MESH,
        )

    @pl.when(tile > 0)
    def _():
        upward().start()

    @pl.when(tile < n - 1)
    def _():
        downward().start()

    @pl.when(tile > 0)
    def _():
        downward().wait_recv()
        first[:, 0:HALO] = halo[0]

    @pl.when(tile == 0)
    def _():
        first[:, 0:HALO] = jnp.zeros_like(first[:, 0:HALO])

    @pl.when(tile < n - 1)
    def _():
        upward().wait_recv()
        first[:, HALO + rows :] = halo[1]

    @pl.when(tile == n - 1)
    def _():
        first[:, HALO + rows :] = jnp.zeros_like(first[:, 0:HALO])

    @pl.when(tile > 0)
    def _():
        upward().wait_send()

    @pl.when(tile < n - 1)
    def _():
        downward().wait_send()


    row_base = tile * rows - HALO
    grid_rows = n * rows

    def sweep(source, low, high, write):
        def chunk(begin, count):
            shape = (2, count + 1, blocks, 128)
            lane = lax.broadcasted_iota(jnp.int32, shape, 3)
            block = lax.broadcasted_iota(jnp.int32, shape, 2)
            row = row_base + begin - 1 + lax.broadcasted_iota(jnp.int32, shape, 1)
            wrap = jnp.where((block == share) & (lane >= 64), 128 * blocks, 0)
            column = group * share * 128 + block * 128 + lane - wrap
            inside = (column >= 0) & (column < NCOL) & (row >= 0) & (row < grid_rows)
            keep_down = jnp.where(inside & (row < grid_rows - 1), 1.0, 0.0)
            keep_right = jnp.where(inside & (column < NCOL - 1), 1.0, 0.0)
            held = source[:, begin - 1 : begin + count + 1, 0:blocks, :]
            here = held[:, :-1]
            following = jnp.concatenate([here[:, :, 1:], here[:, :, :1]], axis=2)
            right = jnp.where(lane == 127, pltpu.roll(following, 127, 3), pltpu.roll(here, 127, 3))
            down = (held[:, 1:] - here) * keep_down
            right = (right - here) * keep_right
            square = jnp.sum(down * down + right * right, axis=0, keepdims=True) + floor_square
            inverse = lax.rsqrt(square)
            down = down * inverse
            right = right * inverse
            preceding = jnp.concatenate([right[:, :, share:], right[:, :, :share]], axis=2)
            left = jnp.where(lane == 0, pltpu.roll(preceding, 1, 3), pltpu.roll(right, 1, 3))
            divergence = (down[:, 1:] - down[:, :-1]) + (right - left)[:, 1:]
            here = here[:, 1:]
            base = first[:, begin : begin + count, 0:blocks, :]
            write(begin, count, here - step_size * (here - base - tv_weight * divergence))

        for begin in range(low, high, 4):
            chunk(begin, min(4, high - begin))

    def write_second(begin, count, value):
        second[:, begin : begin + count, 0:blocks, :] = value

    def write_out(begin, count, value):
        out_ref[:, begin - HALO : begin - HALO + count] = value[:, :, 0:share]

    sweep(first, 1, rows + 2 * HALO - 1, write_second)
    sweep(second, HALO, rows + HALO, write_out)


def body(echoes, pulse_slope, pulse_shift, footprint, band_start, row_phase):
    n = lax.axis_size("tile")
    groups = lax.axis_size("pulse")
    held, pulses = pulse_slope.shape
    rows = band_start.shape[0]
    bins = echoes.shape[3] // 128
    planes = 2 * pulses
    share = KBLOCKS // groups
    values = jnp.concatenate([pulse_slope, pulse_shift], axis=1)
    values = jnp.pad(values, ((0, 0), (0, 16 - 2 * pulses)))
    values = jnp.broadcast_to(values[:, :, None], (held, 16, 128))
    message = jnp.concatenate([echoes.reshape(held, planes * bins, 128), values], axis=1)
    phases = jnp.broadcast_to(row_phase[:, None], (rows, 128))
    table = jnp.asarray(interpolation_table(), BF16)

    vmem = pl.BlockSpec(memory_space=pltpu.VMEM)
    smem = pl.BlockSpec(memory_space=pltpu.SMEM)
    padded = -(-(share + 1) // 8) * 8
    extent = rows + 2 * HALO
    slot = (planes * bins + 16, 128)
    piece = (2 * rows * share + 2 * rows, 128)
    dma = pltpu.SemaphoreType.DMA
    refined = pl.pallas_call(
        functools.partial(kernel, held, pulses, rows, groups, n),
        out_shape=jax.ShapeDtypeStruct((2, rows, share, 128), F32),
        in_specs=[smem, smem, vmem, vmem, vmem],
        out_specs=vmem,
        scratch_shapes=[
            pltpu.VMEM((n,) + slot, BF16),
            pltpu.VMEM((n,) + slot, BF16),
            pltpu.VMEM((planes, bins + 8, 128), F32),
            pltpu.VMEM((2 * planes, 32, 128), F32),
            pltpu.VMEM((planes, rows * QUADS, 512), BF16),
            pltpu.VMEM((planes, rows * QUADS, 512), F32),
            pltpu.VMEM((pulses, 2, 4, 8, 128), F32),
            pltpu.VMEM((pulses, 2, rows, 128), F32),
            pltpu.VMEM((2, rows, 4, 8, 128), F32),
            pltpu.VMEM((2 * rows * KBLOCKS, 128), F32),
            pltpu.VMEM((groups,) + piece, BF16),
            pltpu.VMEM((groups - 1,) + piece, BF16),
            pltpu.VMEM((2, extent, padded, 128), F32),
            pltpu.VMEM((2, extent, padded, 128), F32),
            pltpu.VMEM((2, 2, HALO, padded, 128), F32),
            dma((n,)),
            dma((n,)),
            dma((groups - 1,)),
            dma((groups - 1,)),
            dma((2,)),
            dma((2,)),
        ],
        compiler_params=pltpu.CompilerParams(
            collective_id=0, has_side_effects=True, vmem_limit_bytes=48 * 1024 * 1024
        ),
    )(footprint[0], band_start, message, phases, table)
    return refined.reshape(2, rows, NCOL // groups)


def solution(mesh):
    in_specs = (
        P(("pulse", "tile"), None, None, None),
        P(("pulse", "tile"), None),
        P(("pulse", "tile"), None),
        P("pulse", None, None),
        P("tile"),
        P("tile"),
    )
    out_specs = P(None, "tile", "pulse")
    return jax.shard_map(body, mesh=mesh, in_specs=in_specs, out_specs=out_specs, check_vma=False)
```

```python
import functools

import jax
import jax.numpy as jnp
import numpy as np
from jax import lax
from jax.experimental import pallas as pl
from jax.experimental.pallas import tpu as pltpu
from jax.sharding import PartitionSpec as P

NCOL = 4096
ITERS = 2
KBLOCKS = NCOL // 128
QUADS = KBLOCKS // 4
HALO = ITERS

step_size = 0.5
tv_weight = 0.4
floor_square = 0.25

MESH = pl.DeviceIdType.MESH
F32 = jnp.float32
BF16 = jnp.bfloat16


def interpolation_table():
    columns = np.arange(128)
    position = 3 * columns + 4
    base = position // 4
    f = (position % 4) / 4.0
    weights = [
        (-(f**3) + 2 * f**2 - f) / 2,
        (3 * f**3 - 5 * f**2 + 2) / 2,
        (-3 * f**3 + 4 * f**2 + f) / 2,
        (f**3 - f**2) / 2,
    ]
    table = np.zeros((512, 512), np.float32)
    for q in range(4):
        for shift, weight in zip(range(-1, 3), weights):
            table[96 * q + base + shift, 128 * q + columns] += weight
    return table


def sine_cosine(angle):
    turns = jnp.floor(angle * 0.6366197723675814 + 0.5)
    rest = angle - turns * 1.5703125
    rest = rest - turns * 4.837512969970703125e-4
    rest = rest - turns * 7.549789948768648e-8
    square = rest * rest
    sine = rest + rest * square * (
        -1.6666654611e-1 + square * (8.3321608736e-3 - square * 1.9515295891e-4)
    )
    cosine = (1.0 - 0.5 * square) + square * square * (
        4.166664568298827e-2 + square * (-1.388731625493765e-3 + square * 2.443315711809948e-5)
    )
    quarter = turns - 4.0 * jnp.floor(turns * 0.25)
    odd = (quarter == 1.0) | (quarter == 3.0)
    sine_sign = jnp.where(quarter >= 2.0, -1.0, 1.0)
    cosine_sign = jnp.where((quarter == 1.0) | (quarter == 2.0), -1.0, 1.0)
    return (
        sine_sign * jnp.where(odd, cosine, sine),
        cosine_sign * jnp.where(odd, sine, cosine),
    )


def kernel(
    held,
    pulses,
    rows,
    groups,
    n,
    lists_ref,
    start_ref,
    echo_hbm,
    phase_hbm,
    table_hbm,
    out_ref,
    echo_ref,
    phase_ref,
    table_ref,
    fetch_sems,
    picked,
    got,
    wide,
    lhs,
    product,
    ramp,
    rowturn,
    acc,
    image,
    part,
    got_part,
    first,
    second,
    halo,
    sends,
    recvs,
    part_sends,
    part_recvs,
    halo_sends,
    halo_recvs,
):
    bins = (echo_hbm.shape[1] - 16) // (2 * pulses)
    planes = 2 * pulses
    share = KBLOCKS // groups
    blocks = share + 1
    scale = float(pulses * n * groups) ** -0.5
    group = lax.axis_index("pulse")
    tile = lax.axis_index("tile")
    power = n & (n - 1) == 0

    def partner(d):
        if not power:
            return lax.rem(n + d - tile, n)
        other = tile
        bit = 1
        while bit < n:
            other = other + ((d // bit) % 2) * bit * (1 - 2 * ((tile // bit) % 2))
            bit *= 2
        return other

    fetch_echo = pltpu.make_async_copy(echo_hbm, echo_ref, fetch_sems.at[0])
    fetches = [
        pltpu.make_async_copy(table_hbm, table_ref, fetch_sems.at[1]),
        pltpu.make_async_copy(phase_hbm, phase_ref, fetch_sems.at[2]),
    ]
    barrier = pltpu.get_barrier_semaphore()
    fetch_echo.start()
    for copy in fetches:
        copy.start()
    for d in range(1, groups):
        pl.semaphore_signal(
            barrier, inc=1, device_id={"pulse": lax.rem(group + d, groups)}, device_id_type=MESH
        )
    for d in range(1, n):
        pl.semaphore_signal(
            barrier, inc=1, device_id={"tile": lax.rem(tile + d, n)}, device_id_type=MESH
        )

    def names(strip, number):
        found = lists_ref[strip, 0] == number
        for j in range(1, lists_ref.shape[1]):
            found = found | (lists_ref[strip, j] == number)
        return found

    fetch_echo.wait()

    def pick(d, c):
        other = partner(d)
        block = echo_ref[0]
        for b in range(1, held):
            block = jnp.where(names(other, tile * held + b), echo_ref[b], block)
        picked[d] = block
        return c

    lax.fori_loop(0, n, pick, 0)
    pl.semaphore_wait(barrier, n - 1 + groups - 1)

    def block_copy(d):
        return pltpu.make_async_remote_copy(
            src_ref=picked.at[d],
            dst_ref=got.at[d],
            send_sem=sends.at[d],
            recv_sem=recvs.at[d],
            device_id={"tile": partner(d)},
            device_id_type=MESH,
        )

    def send(i, c):
        block_copy(n - i).start()
        return c

    lax.fori_loop(1, n, send, 0)

    lane = lax.broadcasted_iota(jnp.int32, (8, 128), 1)
    sub = lax.broadcasted_iota(jnp.int32, (8, 128), 0)
    wide[:, bins:, :] = jnp.zeros((planes, wide.shape[1] - bins, 128), F32)
    acc[...] = jnp.zeros_like(acc)
    column_in_quad = (512 * sub + lane).astype(F32)

    def widen(block):
        wide[:, :bins, :] = block[: planes * bins].astype(F32).reshape(planes, bins, 128)

    def gather(pair):
        for plane in range(planes):
            halves = []
            for h in range(2):
                begin = start_ref[2 * pair + h]
                at = begin // 128
                off = begin - 128 * at
                shift = lax.rem(128 - off, 128)
                keep = lane < 128 - off
                ys = [
                    pltpu.roll(wide[plane, pl.ds(at + o, 8, stride=3), :], shift, 1)
                    for o in range(5)
                ]
                halves.append([jnp.where(keep, ys[j], ys[j + 1]) for j in range(4)])
            for j in range(4):
                both = jnp.concatenate([halves[0][j], halves[1][j]], axis=0)
                lhs[plane, pl.ds(pl.multiple_of(16 * pair, 16), 16), 128 * j : 128 * j + 128] = (
                    both.astype(BF16)
                )

    def multiply():
        for plane in range(planes):
            product[plane, :, 0:256] = jnp.dot(
                lhs[plane, :, 0:256], table_ref[0:256, 0:256], preferred_element_type=F32
            )
            product[plane, :, 256:512] = jnp.dot(
                lhs[plane], table_ref[:, 256:512], preferred_element_type=F32
            )

    def phase(d, tail):
        source = partner(d)
        used = names(tile, source * held)
        for b in range(1, held):
            used = used | names(tile, source * held + b)
        weight = jnp.where(used, 1.0, 0.0).astype(F32)
        tail = tail.astype(F32)
        for p in range(pulses):
            slope = tail[p : p + 1]
            shift = tail[pulses + p : pulses + p + 1]
            turn_im, turn_re = sine_cosine(phase_ref[...] * shift)
            rowturn[p, 0] = turn_re
            rowturn[p, 1] = turn_im
            im, re = sine_cosine(column_in_quad * slope)
            step_im, step_re = sine_cosine(jnp.broadcast_to(128.0 * slope, (8, 128)))
            re = re * weight
            im = im * weight
            for q in range(4):
                ramp[p, 0, q] = re
                ramp[p, 1, q] = im
                re, im = re * step_re - im * step_im, re * step_im + im * step_re

    def turn(pair):
        rows_at = [2 * pair, 2 * pair + 1]
        row_turn = [
            [[rowturn[p, part_of, pl.ds(r, 1), :] for part_of in range(2)] for p in range(pulses)]
            for r in rows_at
        ]
        for q in range(4):
            ramps = [[ramp[p, part_of, q] for part_of in range(2)] for p in range(pulses)]
            for h, r in enumerate(rows_at):
                at = pl.ds(pl.multiple_of(8 * r, 8), 8)
                total_re = acc[0, r, q]
                total_im = acc[1, r, q]
                for p in range(pulses):
                    row_re, row_im = row_turn[h][p]
                    ramp_re, ramp_im = ramps[p]
                    re = ramp_re * row_re - ramp_im * row_im
                    im = ramp_re * row_im + ramp_im * row_re
                    value_re = product[2 * p, at, 128 * q : 128 * q + 128]
                    value_im = product[2 * p + 1, at, 128 * q : 128 * q + 128]
                    total_re = total_re + (value_re * re - value_im * im)
                    total_im = total_im + (value_re * im + value_im * re)
                acc[0, r, q] = total_re
                acc[1, r, q] = total_im

    def gather_only(pair, c):
        gather(pair)
        return c

    def gather_and_turn(pair, c):
        gather(pair)
        turn(pair)
        return c

    def turn_only(pair, c):
        turn(pair)
        return c

    tail_rows = slice(planes * bins, planes * bins + 16)
    widen(picked[0])
    lax.fori_loop(0, rows // 2, gather_only, 0, unroll=2)
    for copy in fetches:
        copy.wait()
    multiply()
    phase(0, picked[0, tail_rows])

    def slot(d, c):
        block_copy(d).wait_recv()
        widen(got[d])
        lax.fori_loop(0, rows // 2, gather_and_turn, 0, unroll=2)
        multiply()
        phase(d, got[d, tail_rows])
        return c

    lax.fori_loop(1, n, slot, 0)
    lax.fori_loop(0, rows // 2, turn_only, 0, unroll=2)

    def sent(d, c):
        block_copy(d).wait_send()
        return c

    lax.fori_loop(1, n, sent, 0)

    def place(r, c):
        for plane in range(2):
            for q in range(4):
                image[pl.ds((plane * rows + r) * KBLOCKS + q, QUADS, stride=4), :] = (
                    acc[plane, r, q] * scale
                )
        return c

    lax.fori_loop(0, rows, place, 0, unroll=2)

    together = 16 // share
    main = 2 * rows * share
    wide_lane = lax.broadcasted_iota(jnp.int32, (rows, 128), 1)

    def emit_for(g):
        def emit(i, c):
            parts = [
                image[pl.ds((i * together + h) * KBLOCKS + share * g, share), :]
                for h in range(together)
            ]
            part[g, pl.ds(pl.multiple_of(16 * i, 16), 16), :] = jnp.concatenate(
                parts, axis=0
            ).astype(BF16)
            return c

        lax.fori_loop(0, 2 * rows // together, emit, 0, unroll=4)
        after = jnp.minimum(share * (g + 1), KBLOCKS - 1)
        before = jnp.maximum(share * g - 1, 0)
        for plane in range(2):
            edge = jnp.where(
                wide_lane < 64,
                image[pl.ds(plane * rows * KBLOCKS + after, rows, stride=KBLOCKS), :],
                image[pl.ds(plane * rows * KBLOCKS + before, rows, stride=KBLOCKS), :],
            )
            part[g, main + plane * rows : main + (plane + 1) * rows, :] = edge.astype(BF16)

    copies = []
    for d in range(groups - 1, 0, -1):
        target = lax.rem(group + d, groups)
        emit_for(target)
        copy = pltpu.make_async_remote_copy(
            src_ref=part.at[target],
            dst_ref=got_part.at[d - 1],
            send_sem=part_sends.at[d - 1],
            recv_sem=part_recvs.at[d - 1],
            device_id={"pulse": target},
            device_id_type=MESH,
        )
        copy.start()
        copies.append(copy)
    emit_for(group)
    for copy in copies:
        copy.wait()

    total = part[group].astype(F32)
    for d in range(1, groups):
        total = total + got_part[d - 1].astype(F32)
    for plane in range(2):
        first[plane, HALO : HALO + rows, 0:share, :] = total[
            plane * rows * share : (plane + 1) * rows * share
        ].reshape(rows, share, 128)
        for r in range(rows):
            at = main + plane * rows + r
            first[plane, HALO + r, share:blocks, :] = total[at : at + 1]

    def upward():
        return pltpu.make_async_remote_copy(
            src_ref=first.at[:, pl.ds(HALO, HALO)],
            dst_ref=halo.at[1],
            send_sem=halo_sends.at[1],
            recv_sem=halo_recvs.at[1],
            device_id={"tile": tile - 1},
            device_id_type=MESH,
        )

    def downward():
        return pltpu.make_async_remote_copy(
            src_ref=first.at[:, pl.ds(rows, HALO)],
            dst_ref=halo.at[0],
            send_sem=halo_sends.at[0],
            recv_sem=halo_recvs.at[0],
            device_id={"tile": tile + 1},
            device_id_type=MESH,
        )

    @pl.when(tile > 0)
    def _():
        upward().start()

    @pl.when(tile < n - 1)
    def _():
        downward().start()

    @pl.when(tile > 0)
    def _():
        downward().wait_recv()
        first[:, 0:HALO] = halo[0]

    @pl.when(tile == 0)
    def _():
        first[:, 0:HALO] = jnp.zeros_like(first[:, 0:HALO])

    @pl.when(tile < n - 1)
    def _():
        upward().wait_recv()
        first[:, HALO + rows :] = halo[1]

    @pl.when(tile == n - 1)
    def _():
        first[:, HALO + rows :] = jnp.zeros_like(first[:, 0:HALO])

    @pl.when(tile > 0)
    def _():
        upward().wait_send()

    @pl.when(tile < n - 1)
    def _():
        downward().wait_send()


    row_base = tile * rows - HALO
    grid_rows = n * rows

    def sweep(source, low, high, write):
        def chunk(begin, count):
            shape = (2, count + 1, blocks, 128)
            lane = lax.broadcasted_iota(jnp.int32, shape, 3)
            block = lax.broadcasted_iota(jnp.int32, shape, 2)
            row = row_base + begin - 1 + lax.broadcasted_iota(jnp.int32, shape, 1)
            wrap = jnp.where((block == share) & (lane >= 64), 128 * blocks, 0)
            column = group * share * 128 + block * 128 + lane - wrap
            inside = (column >= 0) & (column < NCOL) & (row >= 0) & (row < grid_rows)
            keep_down = jnp.where(inside & (row < grid_rows - 1), 1.0, 0.0)
            keep_right = jnp.where(inside & (column < NCOL - 1), 1.0, 0.0)
            held = source[:, begin - 1 : begin + count + 1, 0:blocks, :]
            here = held[:, :-1]
            following = jnp.concatenate([here[:, :, 1:], here[:, :, :1]], axis=2)
            right = jnp.where(lane == 127, pltpu.roll(following, 127, 3), pltpu.roll(here, 127, 3))
            down = (held[:, 1:] - here) * keep_down
            right = (right - here) * keep_right
            square = jnp.sum(down * down + right * right, axis=0, keepdims=True) + floor_square
            inverse = lax.rsqrt(square)
            down = down * inverse
            right = right * inverse
            preceding = jnp.concatenate([right[:, :, share:], right[:, :, :share]], axis=2)
            left = jnp.where(lane == 0, pltpu.roll(preceding, 1, 3), pltpu.roll(right, 1, 3))
            divergence = (down[:, 1:] - down[:, :-1]) + (right - left)[:, 1:]
            here = here[:, 1:]
            base = first[:, begin : begin + count, 0:blocks, :]
            write(begin, count, here - step_size * (here - base - tv_weight * divergence))

        for begin in range(low, high, 4):
            chunk(begin, min(4, high - begin))

    def write_second(begin, count, value):
        second[:, begin : begin + count, 0:blocks, :] = value

    def write_out(begin, count, value):
        out_ref[:, begin - HALO : begin - HALO + count] = value[:, :, 0:share]

    sweep(first, 1, rows + 2 * HALO - 1, write_second)
    sweep(second, HALO, rows + HALO, write_out)


def body(echoes, pulse_slope, pulse_shift, footprint, band_start, row_phase):
    n = lax.axis_size("tile")
    groups = lax.axis_size("pulse")
    held, pulses = pulse_slope.shape
    rows = band_start.shape[0]
    bins = echoes.shape[3] // 128
    planes = 2 * pulses
    share = KBLOCKS // groups
    values = jnp.concatenate([pulse_slope, pulse_shift], axis=1)
    values = jnp.pad(values, ((0, 0), (0, 16 - 2 * pulses)))
    values = jnp.broadcast_to(values[:, :, None], (held, 16, 128))
    message = jnp.concatenate([echoes.reshape(held, planes * bins, 128), values], axis=1)
    phases = jnp.broadcast_to(row_phase[:, None], (rows, 128))
    table = jnp.asarray(interpolation_table(), BF16)

    vmem = pl.BlockSpec(memory_space=pltpu.VMEM)
    smem = pl.BlockSpec(memory_space=pltpu.SMEM)
    anywhere = pl.BlockSpec(memory_space=pl.ANY)
    padded = -(-(share + 1) // 8) * 8
    extent = rows + 2 * HALO
    slot = (planes * bins + 16, 128)
    piece = (2 * rows * share + 2 * rows, 128)
    dma = pltpu.SemaphoreType.DMA
    refined = pl.pallas_call(
        functools.partial(kernel, held, pulses, rows, groups, n),
        out_shape=jax.ShapeDtypeStruct((2, rows, share, 128), F32),
        in_specs=[smem, smem, anywhere, anywhere, anywhere],
        out_specs=vmem,
        scratch_shapes=[
            pltpu.VMEM(message.shape, BF16),
            pltpu.VMEM(phases.shape, F32),
            pltpu.VMEM(table.shape, BF16),
            dma((3,)),
            pltpu.VMEM((n,) + slot, BF16),
            pltpu.VMEM((n,) + slot, BF16),
            pltpu.VMEM((planes, bins + 8, 128), F32),
            pltpu.VMEM((planes, rows * QUADS, 512), BF16),
            pltpu.VMEM((planes, rows * QUADS, 512), F32),
            pltpu.VMEM((pulses, 2, 4, 8, 128), F32),
            pltpu.VMEM((pulses, 2, rows, 128), F32),
            pltpu.VMEM((2, rows, 4, 8, 128), F32),
            pltpu.VMEM((2 * rows * KBLOCKS, 128), F32),
            pltpu.VMEM((groups,) + piece, BF16),
            pltpu.VMEM((groups - 1,) + piece, BF16),
            pltpu.VMEM((2, extent, padded, 128), F32),
            pltpu.VMEM((2, extent, padded, 128), F32),
            pltpu.VMEM((2, 2, HALO, padded, 128), F32),
            dma((n,)),
            dma((n,)),
            dma((groups - 1,)),
            dma((groups - 1,)),
            dma((2,)),
            dma((2,)),
        ],
        compiler_params=pltpu.CompilerParams(
            collective_id=0, has_side_effects=True, vmem_limit_bytes=48 * 1024 * 1024
        ),
    )(footprint[0], band_start, message, phases, table)
    return refined.reshape(2, rows, NCOL // groups)


def solution(mesh):
    in_specs = (
        P(("pulse", "tile"), None, None, None),
        P(("pulse", "tile"), None),
        P(("pulse", "tile"), None),
        P("pulse", None, None),
        P("tile"),
        P("tile"),
    )
    out_specs = P(None, "tile", "pulse")
    return jax.shard_map(body, mesh=mesh, in_specs=in_specs, out_specs=out_specs, check_vma=False)
```

```python
import functools

import jax
import jax.numpy as jnp
import numpy as np
from jax import lax
from jax.experimental import pallas as pl
from jax.experimental.pallas import tpu as pltpu
from jax.sharding import PartitionSpec as P

NCOL = 4096
ITERS = 2
KBLOCKS = NCOL // 128
QUADS = KBLOCKS // 4
HALO = ITERS

step_size = 0.5
tv_weight = 0.4
floor_square = 0.25

MESH = pl.DeviceIdType.MESH
F32 = jnp.float32
BF16 = jnp.bfloat16


def interpolation_table():
    columns = np.arange(128)
    position = 3 * columns + 4
    base = position // 4
    f = (position % 4) / 4.0
    weights = [
        (-(f**3) + 2 * f**2 - f) / 2,
        (3 * f**3 - 5 * f**2 + 2) / 2,
        (-3 * f**3 + 4 * f**2 + f) / 2,
        (f**3 - f**2) / 2,
    ]
    table = np.zeros((512, 512), np.float32)
    for q in range(4):
        for shift, weight in zip(range(-1, 3), weights):
            table[96 * q + base + shift, 128 * q + columns] += weight
    return table


def sine_cosine(angle):
    turns = jnp.floor(angle * 0.6366197723675814 + 0.5)
    rest = angle - turns * 1.5703125
    rest = rest - turns * 4.837512969970703125e-4
    rest = rest - turns * 7.549789948768648e-8
    square = rest * rest
    sine = rest + rest * square * (
        -1.6666654611e-1 + square * (8.3321608736e-3 - square * 1.9515295891e-4)
    )
    cosine = (1.0 - 0.5 * square) + square * square * (
        4.166664568298827e-2 + square * (-1.388731625493765e-3 + square * 2.443315711809948e-5)
    )
    quarter = turns - 4.0 * jnp.floor(turns * 0.25)
    odd = (quarter == 1.0) | (quarter == 3.0)
    sine_sign = jnp.where(quarter >= 2.0, -1.0, 1.0)
    cosine_sign = jnp.where((quarter == 1.0) | (quarter == 2.0), -1.0, 1.0)
    return (
        sine_sign * jnp.where(odd, cosine, sine),
        cosine_sign * jnp.where(odd, sine, cosine),
    )


NEAR, FAR = 0, 1


def kernel(
    held,
    pulses,
    rows,
    groups,
    n,
    lists_ref,
    starts_hbm,
    echo_hbm,
    phase_hbm,
    table_hbm,
    out_ref,
    starts_far,
    starts,
    phase_ref,
    table_ref,
    got,
    wide,
    lhs,
    product,
    ramp,
    rowturn,
    acc,
    image,
    part,
    got_part,
    far_out,
    far_in,
    first,
    second,
    halo,
    fetch_sems,
    info_sends,
    info_recvs,
    sends,
    recvs,
    part_sends,
    part_recvs,
    far_sends,
    far_recvs,
    halo_sends,
    halo_recvs,
):
    planes = 2 * pulses
    bins = (echo_hbm.shape[1] - 16) // planes
    share = KBLOCKS // groups
    blocks = share + 1
    scale = float(pulses * n * groups) ** -0.5
    group = lax.axis_index("pulse")
    tile = lax.axis_index("tile")
    half = n // 2
    far_tile = lax.rem(tile + half, n)
    local = lax.rem(tile, half)
    base_tile = tile - local
    power = half & (half - 1) == 0

    def partner(d):
        if not power:
            return base_tile + lax.rem(half + d - local, half)
        other = tile
        bit = 1
        while bit < half:
            other = other + ((d // bit) % 2) * bit * (1 - 2 * ((tile // bit) % 2))
            bit *= 2
        return other

    fetches = [
        pltpu.make_async_copy(starts_hbm, starts.at[NEAR], fetch_sems.at[0]),
        pltpu.make_async_copy(phase_hbm, phase_ref.at[NEAR], fetch_sems.at[1]),
        pltpu.make_async_copy(echo_hbm, got.at[0], fetch_sems.at[2]),
        pltpu.make_async_copy(table_hbm, table_ref, fetch_sems.at[3]),
    ]
    barrier = pltpu.get_barrier_semaphore()
    for copy in fetches:
        copy.start()
    for d in range(1, groups):
        pl.semaphore_signal(
            barrier, inc=1, device_id={"pulse": lax.rem(group + d, groups)}, device_id_type=MESH
        )
    for d in range(1, n):
        pl.semaphore_signal(
            barrier, inc=1, device_id={"tile": lax.rem(tile + d, n)}, device_id_type=MESH
        )

    def names(strip, number):
        found = lists_ref[strip, 0] == number
        for j in range(1, lists_ref.shape[1]):
            found = found | (lists_ref[strip, j] == number)
        return found

    pl.semaphore_wait(barrier, n - 1 + groups - 1)

    def remote(src, dst, send_sem, recv_sem, target):
        return pltpu.make_async_remote_copy(
            src_ref=src,
            dst_ref=dst,
            send_sem=send_sem,
            recv_sem=recv_sem,
            device_id=target,
            device_id_type=MESH,
        )

    infos = [
        remote(src, dst, info_sends.at[j], info_recvs.at[j], {"tile": far_tile})
        for j, (src, dst) in enumerate(
            ((starts_hbm, starts_far), (phase_hbm, phase_ref.at[FAR]))
        )
    ]
    for copy in infos:
        copy.start()

    def block_copy(d):
        return remote(echo_hbm, got.at[d], sends.at[d], recvs.at[d], {"tile": partner(d)})

    def send(d, c):
        block_copy(d).start()
        return c

    lax.fori_loop(1, half, send, 0)

    lane = lax.broadcasted_iota(jnp.int32, (8, 128), 1)
    sub = lax.broadcasted_iota(jnp.int32, (8, 128), 0)
    wide[:, bins:, :] = jnp.zeros((planes, wide.shape[1] - bins, 128), F32)
    acc[...] = jnp.zeros_like(acc)
    strip_tile = (tile, far_tile)
    column_in_quad = (512 * sub + lane).astype(F32)

    def chosen(strip, d, at):
        number = partner(d) * held
        block = got[d, 0, at]
        for b in range(1, held):
            block = jnp.where(names(strip_tile[strip], number + b), got[d, b, at], block)
        return block

    def widen(strip, d):
        block = chosen(strip, d, slice(0, planes * bins))
        wide[:, :bins, :] = block.astype(F32).reshape(planes, bins, 128)

    def gather(strip, pair):
        for plane in range(planes):
            halves = []
            for h in range(2):
                row = 2 * pair + h
                begin = starts[strip, row // 128, lax.rem(row, 128)]
                at = begin // 128
                off = begin - 128 * at
                shift = lax.rem(128 - off, 128)
                keep = lane < 128 - off
                ys = [
                    pltpu.roll(wide[plane, pl.ds(at + o, 8, stride=3), :], shift, 1)
                    for o in range(5)
                ]
                halves.append([jnp.where(keep, ys[j], ys[j + 1]) for j in range(4)])
            for j in range(4):
                both = jnp.concatenate([halves[0][j], halves[1][j]], axis=0)
                lhs[plane, pl.ds(pl.multiple_of(16 * pair, 16), 16), 128 * j : 128 * j + 128] = (
                    both.astype(BF16)
                )

    def multiply():
        for plane in range(planes):
            product[plane, :, 0:256] = jnp.dot(
                lhs[plane, :, 0:256], table_ref[0:256, 0:256], preferred_element_type=F32
            )
            product[plane, :, 256:512] = jnp.dot(
                lhs[plane], table_ref[:, 256:512], preferred_element_type=F32
            )

    def phase(strip, d):
        tail = chosen(strip, d, slice(planes * bins, planes * bins + 16))
        number = partner(d) * held
        used = names(strip_tile[strip], number)
        for b in range(1, held):
            used = used | names(strip_tile[strip], number + b)
        weight = jnp.where(used, 1.0, 0.0).astype(F32)
        tail = tail.astype(F32)
        for p in range(pulses):
            slope = tail[p : p + 1]
            shift = tail[pulses + p : pulses + p + 1]
            turn_im, turn_re = sine_cosine(phase_ref[strip] * shift)
            rowturn[p, 0] = turn_re
            rowturn[p, 1] = turn_im
            im, re = sine_cosine(column_in_quad * slope)
            step_im, step_re = sine_cosine(jnp.broadcast_to(128.0 * slope, (8, 128)))
            re = re * weight
            im = im * weight
            for q in range(4):
                ramp[p, 0, q] = re
                ramp[p, 1, q] = im
                re, im = re * step_re - im * step_im, re * step_im + im * step_re

    def turn(strip, pair):
        rows_at = [2 * pair, 2 * pair + 1]
        row_turn = [
            [[rowturn[p, part_of, pl.ds(r, 1), :] for part_of in range(2)] for p in range(pulses)]
            for r in rows_at
        ]
        for q in range(4):
            ramps = [[ramp[p, part_of, q] for part_of in range(2)] for p in range(pulses)]
            for h, r in enumerate(rows_at):
                at = pl.ds(pl.multiple_of(8 * r, 8), 8)
                total_re = acc[strip, 0, r, q]
                total_im = acc[strip, 1, r, q]
                for p in range(pulses):
                    row_re, row_im = row_turn[h][p]
                    ramp_re, ramp_im = ramps[p]
                    re = ramp_re * row_re - ramp_im * row_im
                    im = ramp_re * row_im + ramp_im * row_re
                    value_re = product[2 * p, at, 128 * q : 128 * q + 128]
                    value_im = product[2 * p + 1, at, 128 * q : 128 * q + 128]
                    total_re = total_re + (value_re * re - value_im * im)
                    total_im = total_im + (value_re * im + value_im * re)
                acc[strip, 0, r, q] = total_re
                acc[strip, 1, r, q] = total_im

    def rows_loop(gathered, turned):
        def step(pair, c):
            if gathered is not None:
                gather(gathered, pair)
            if turned is not None:
                turn(turned, pair)
            return c

        lax.fori_loop(0, rows // 2, step, 0, unroll=2)

    def arrive(d):
        block_copy(d).wait_recv()

    def finish(strip, d):
        multiply()
        phase(strip, d)

    def part_copy(strip, d):
        target = lax.rem(group + d, groups)
        return remote(
            part.at[strip, target],
            got_part.at[strip, d - 1],
            part_sends.at[strip, d - 1],
            part_recvs.at[strip, d - 1],
            {"pulse": target},
        )

    together = 16 // share
    main = 2 * rows * share
    wide_lane = lax.broadcasted_iota(jnp.int32, (rows, 128), 1)

    def emit_strip(strip):
        def place(r, c):
            for plane in range(2):
                for q in range(4):
                    image[pl.ds((plane * rows + r) * KBLOCKS + q, QUADS, stride=4), :] = (
                        acc[strip, plane, r, q] * scale
                    )
            return c

        lax.fori_loop(0, rows, place, 0, unroll=4)

        def emit_for(g):
            def emit(i, c):
                parts = [
                    image[pl.ds((i * together + h) * KBLOCKS + share * g, share), :]
                    for h in range(together)
                ]
                part[strip, g, pl.ds(pl.multiple_of(16 * i, 16), 16), :] = jnp.concatenate(
                    parts, axis=0
                ).astype(BF16)
                return c

            lax.fori_loop(0, 2 * rows // together, emit, 0, unroll=4)
            after = jnp.minimum(share * (g + 1), KBLOCKS - 1)
            before = jnp.maximum(share * g - 1, 0)
            for plane in range(2):
                edge = jnp.where(
                    wide_lane < 64,
                    image[pl.ds(plane * rows * KBLOCKS + after, rows, stride=KBLOCKS), :],
                    image[pl.ds(plane * rows * KBLOCKS + before, rows, stride=KBLOCKS), :],
                )
                part[strip, g, main + plane * rows : main + (plane + 1) * rows, :] = edge.astype(
                    BF16
                )

        for d in range(groups - 1, 0, -1):
            emit_for(lax.rem(group + d, groups))
            part_copy(strip, d).start()
        emit_for(group)

    def summed(strip):
        for d in range(1, groups):
            part_copy(strip, d).wait_recv()
        total = part[strip, group].astype(F32)
        for d in range(1, groups):
            total = total + got_part[strip, d - 1].astype(F32)
        return total

    for copy in fetches[:3]:
        copy.wait()
    widen(NEAR, 0)
    rows_loop(NEAR, None)
    fetches[3].wait()
    finish(NEAR, 0)

    for copy in infos:
        copy.wait_recv()
    far_starts = pltpu.make_async_copy(starts_far, starts.at[FAR], fetch_sems.at[0])
    far_starts.start()
    widen(FAR, 0)
    far_starts.wait()
    rows_loop(FAR, NEAR)
    finish(FAR, 0)

    def far_slot(d, c):
        arrive(d)
        widen(FAR, d)
        rows_loop(FAR, FAR)
        finish(FAR, d)
        return c

    lax.fori_loop(1, half, far_slot, 0)

    widen(NEAR, 1)
    rows_loop(NEAR, FAR)
    emit_strip(FAR)
    finish(NEAR, 1)

    def near_slot(d, c):
        widen(NEAR, d)
        rows_loop(NEAR, NEAR)
        finish(NEAR, d)
        return c

    lax.fori_loop(2, half, near_slot, 0)
    rows_loop(None, NEAR)
    emit_strip(NEAR)

    far_out[...] = summed(FAR).astype(BF16)
    cross = remote(far_out, far_in, far_sends.at[0], far_recvs.at[0], {"tile": far_tile})
    cross.start()
    total = summed(NEAR)
    cross.wait_recv()
    total = total + far_in[...].astype(F32)
    for plane in range(2):
        first[plane, HALO : HALO + rows, 0:share, :] = total[
            plane * rows * share : (plane + 1) * rows * share
        ].reshape(rows, share, 128)
        for r in range(rows):
            at = main + plane * rows + r
            first[plane, HALO + r, share:blocks, :] = total[at : at + 1]

    def upward():
        return pltpu.make_async_remote_copy(
            src_ref=first.at[:, pl.ds(HALO, HALO)],
            dst_ref=halo.at[1],
            send_sem=halo_sends.at[1],
            recv_sem=halo_recvs.at[1],
            device_id={"tile": tile - 1},
            device_id_type=MESH,
        )

    def downward():
        return pltpu.make_async_remote_copy(
            src_ref=first.at[:, pl.ds(rows, HALO)],
            dst_ref=halo.at[0],
            send_sem=halo_sends.at[0],
            recv_sem=halo_recvs.at[0],
            device_id={"tile": tile + 1},
            device_id_type=MESH,
        )

    @pl.when(tile > 0)
    def _():
        upward().start()

    @pl.when(tile < n - 1)
    def _():
        downward().start()

    @pl.when(tile > 0)
    def _():
        downward().wait_recv()
        first[:, 0:HALO] = halo[0]

    @pl.when(tile == 0)
    def _():
        first[:, 0:HALO] = jnp.zeros_like(first[:, 0:HALO])

    @pl.when(tile < n - 1)
    def _():
        upward().wait_recv()
        first[:, HALO + rows :] = halo[1]

    @pl.when(tile == n - 1)
    def _():
        first[:, HALO + rows :] = jnp.zeros_like(first[:, 0:HALO])

    @pl.when(tile > 0)
    def _():
        upward().wait_send()

    @pl.when(tile < n - 1)
    def _():
        downward().wait_send()


    row_base = tile * rows - HALO
    grid_rows = n * rows

    def sweep(source, low, high, write):
        def chunk(begin, count):
            shape = (2, count + 1, blocks, 128)
            lane = lax.broadcasted_iota(jnp.int32, shape, 3)
            block = lax.broadcasted_iota(jnp.int32, shape, 2)
            row = row_base + begin - 1 + lax.broadcasted_iota(jnp.int32, shape, 1)
            wrap = jnp.where((block == share) & (lane >= 64), 128 * blocks, 0)
            column = group * share * 128 + block * 128 + lane - wrap
            inside = (column >= 0) & (column < NCOL) & (row >= 0) & (row < grid_rows)
            keep_down = jnp.where(inside & (row < grid_rows - 1), 1.0, 0.0)
            keep_right = jnp.where(inside & (column < NCOL - 1), 1.0, 0.0)
            held = source[:, begin - 1 : begin + count + 1, 0:blocks, :]
            here = held[:, :-1]
            following = jnp.concatenate([here[:, :, 1:], here[:, :, :1]], axis=2)
            right = jnp.where(lane == 127, pltpu.roll(following, 127, 3), pltpu.roll(here, 127, 3))
            down = (held[:, 1:] - here) * keep_down
            right = (right - here) * keep_right
            square = jnp.sum(down * down + right * right, axis=0, keepdims=True) + floor_square
            inverse = lax.rsqrt(square)
            down = down * inverse
            right = right * inverse
            preceding = jnp.concatenate([right[:, :, share:], right[:, :, :share]], axis=2)
            left = jnp.where(lane == 0, pltpu.roll(preceding, 1, 3), pltpu.roll(right, 1, 3))
            divergence = (down[:, 1:] - down[:, :-1]) + (right - left)[:, 1:]
            here = here[:, 1:]
            base = first[:, begin : begin + count, 0:blocks, :]
            write(begin, count, here - step_size * (here - base - tv_weight * divergence))

        for begin in range(low, high, 4):
            chunk(begin, min(4, high - begin))

    def write_second(begin, count, value):
        second[:, begin : begin + count, 0:blocks, :] = value

    def write_out(begin, count, value):
        out_ref[:, begin - HALO : begin - HALO + count] = value[:, :, 0:share]

    sweep(first, 1, rows + 2 * HALO - 1, write_second)
    sweep(second, HALO, rows + HALO, write_out)

    def sent(d, c):
        block_copy(d).wait_send()
        return c

    lax.fori_loop(1, half, sent, 0)
    for copy in infos:
        copy.wait_send()
    cross.wait_send()
    for strip in (NEAR, FAR):
        for d in range(1, groups):
            part_copy(strip, d).wait_send()


def body(echoes, pulse_slope, pulse_shift, footprint, band_start, row_phase):
    n = lax.axis_size("tile")
    groups = lax.axis_size("pulse")
    held, pulses = pulse_slope.shape
    rows = band_start.shape[0]
    bins = echoes.shape[3] // 128
    planes = 2 * pulses
    share = KBLOCKS // groups
    values = jnp.concatenate([pulse_slope, pulse_shift], axis=1)
    values = jnp.pad(values, ((0, 0), (0, 16 - 2 * pulses)))
    values = jnp.broadcast_to(values[:, :, None], (held, 16, 128))
    message = jnp.concatenate([echoes.reshape(held, planes * bins, 128), values], axis=1)
    phases = jnp.broadcast_to(row_phase[:, None], (rows, 128))
    start_rows = 8 * (-(-rows // 1024))
    starts = jnp.pad(band_start, (0, 128 * start_rows - rows)).reshape(start_rows, 128)
    table = jnp.asarray(interpolation_table(), BF16)

    vmem = pl.BlockSpec(memory_space=pltpu.VMEM)
    smem = pl.BlockSpec(memory_space=pltpu.SMEM)
    anywhere = pl.BlockSpec(memory_space=pl.ANY)
    padded = -(-(share + 1) // 8) * 8
    extent = rows + 2 * HALO
    piece = (2 * rows * share + 2 * rows, 128)
    dma = pltpu.SemaphoreType.DMA
    refined = pl.pallas_call(
        functools.partial(kernel, held, pulses, rows, groups, n),
        out_shape=jax.ShapeDtypeStruct((2, rows, share, 128), F32),
        in_specs=[smem, anywhere, anywhere, anywhere, anywhere],
        out_specs=vmem,
        scratch_shapes=[
            pltpu.VMEM(starts.shape, jnp.int32),
            pltpu.SMEM((2,) + starts.shape, jnp.int32),
            pltpu.VMEM((2,) + phases.shape, F32),
            pltpu.VMEM(table.shape, BF16),
            pltpu.VMEM((n // 2,) + message.shape, BF16),
            pltpu.VMEM((planes, bins + 8, 128), F32),
            pltpu.VMEM((planes, rows * QUADS, 512), BF16),
            pltpu.VMEM((planes, rows * QUADS, 512), F32),
            pltpu.VMEM((pulses, 2, 4, 8, 128), F32),
            pltpu.VMEM((pulses, 2, rows, 128), F32),
            pltpu.VMEM((2, 2, rows, 4, 8, 128), F32),
            pltpu.VMEM((2 * rows * KBLOCKS, 128), F32),
            pltpu.VMEM((2, groups) + piece, BF16),
            pltpu.VMEM((2, groups - 1) + piece, BF16),
            pltpu.VMEM(piece, BF16),
            pltpu.VMEM(piece, BF16),
            pltpu.VMEM((2, extent, padded, 128), F32),
            pltpu.VMEM((2, extent, padded, 128), F32),
            pltpu.VMEM((2, 2, HALO, padded, 128), F32),
            dma((4,)),
            dma((2,)),
            dma((2,)),
            dma((n // 2,)),
            dma((n // 2,)),
            dma((2, groups - 1)),
            dma((2, groups - 1)),
            dma((1,)),
            dma((1,)),
            dma((2,)),
            dma((2,)),
        ],
        compiler_params=pltpu.CompilerParams(
            collective_id=0, has_side_effects=True, vmem_limit_bytes=48 * 1024 * 1024
        ),
    )(footprint[0], starts, message, phases, table)
    return refined.reshape(2, rows, NCOL // groups)


def solution(mesh):
    in_specs = (
        P(("pulse", "tile"), None, None, None),
        P(("pulse", "tile"), None),
        P(("pulse", "tile"), None),
        P("pulse", None, None),
        P("tile"),
        P("tile"),
    )
    out_specs = P(None, "tile", "pulse")
    return jax.shard_map(body, mesh=mesh, in_specs=in_specs, out_specs=out_specs, check_vma=False)
```

```python
import functools

import jax
import jax.numpy as jnp
import numpy as np
from jax import lax
from jax.experimental import pallas as pl
from jax.experimental.pallas import tpu as pltpu
from jax.sharding import PartitionSpec as P

NCOL = 4096
ITERS = 2
KBLOCKS = NCOL // 128
QUADS = KBLOCKS // 4
HALO = ITERS

step_size = 0.5
tv_weight = 0.4
floor_square = 0.25

MESH = pl.DeviceIdType.MESH
F32 = jnp.float32
BF16 = jnp.bfloat16


def interpolation_table():
    columns = np.arange(128)
    position = 3 * columns + 4
    base = position // 4
    f = (position % 4) / 4.0
    weights = [
        (-(f**3) + 2 * f**2 - f) / 2,
        (3 * f**3 - 5 * f**2 + 2) / 2,
        (-3 * f**3 + 4 * f**2 + f) / 2,
        (f**3 - f**2) / 2,
    ]
    table = np.zeros((512, 512), np.float32)
    for q in range(4):
        for shift, weight in zip(range(-1, 3), weights):
            table[96 * q + base + shift, 128 * q + columns] += weight
    return table


def sine_cosine(angle):
    turns = jnp.floor(angle * 0.6366197723675814 + 0.5)
    rest = angle - turns * 1.5703125
    rest = rest - turns * 4.837512969970703125e-4
    rest = rest - turns * 7.549789948768648e-8
    square = rest * rest
    sine = rest + rest * square * (
        -1.6666654611e-1 + square * (8.3321608736e-3 - square * 1.9515295891e-4)
    )
    cosine = (1.0 - 0.5 * square) + square * square * (
        4.166664568298827e-2 + square * (-1.388731625493765e-3 + square * 2.443315711809948e-5)
    )
    quarter = turns - 4.0 * jnp.floor(turns * 0.25)
    odd = (quarter == 1.0) | (quarter == 3.0)
    sine_sign = jnp.where(quarter >= 2.0, -1.0, 1.0)
    cosine_sign = jnp.where((quarter == 1.0) | (quarter == 2.0), -1.0, 1.0)
    return (
        sine_sign * jnp.where(odd, cosine, sine),
        cosine_sign * jnp.where(odd, sine, cosine),
    )


NEAR, FAR = 0, 1


def kernel(
    held,
    pulses,
    rows,
    groups,
    n,
    lists_hbm,
    starts_hbm,
    echo_hbm,
    slope_hbm,
    shift_hbm,
    phase_hbm,
    table_hbm,
    out_ref,
    lists_ref,
    starts_far,
    starts,
    slope_ref,
    shift_ref,
    phase_line,
    phase_ref,
    table_ref,
    values,
    got_values,
    got,
    wide,
    lhs,
    product,
    ramp,
    rowturn,
    acc,
    part,
    got_part,
    far_out,
    far_in,
    first,
    second,
    halo_out,
    halo,
    fetch_sems,
    info_sends,
    info_recvs,
    sends,
    recvs,
    value_sends,
    value_recvs,
    part_sends,
    part_recvs,
    far_sends,
    far_recvs,
    halo_sends,
    halo_recvs,
):
    planes = 2 * pulses
    bins = echo_hbm.shape[1] // planes
    share = KBLOCKS // groups
    blocks = share + 1
    scale = float(pulses * n * groups) ** -0.5
    group = lax.axis_index("pulse")
    tile = lax.axis_index("tile")
    half = n // 2
    far_tile = lax.rem(tile + half, n)
    local = lax.rem(tile, half)
    base_tile = tile - local
    power = half & (half - 1) == 0

    def partner(d):
        if not power:
            return base_tile + lax.rem(half + d - local, half)
        other = tile
        bit = 1
        while bit < half:
            other = other + ((d // bit) % 2) * bit * (1 - 2 * ((tile // bit) % 2))
            bit *= 2
        return other

    fetches = [
        pltpu.make_async_copy(slope_hbm, slope_ref, fetch_sems.at[0]),
        pltpu.make_async_copy(shift_hbm, shift_ref, fetch_sems.at[1]),
        pltpu.make_async_copy(starts_hbm, starts.at[NEAR], fetch_sems.at[2]),
        pltpu.make_async_copy(phase_hbm, phase_line.at[NEAR], fetch_sems.at[3]),
        pltpu.make_async_copy(lists_hbm, lists_ref, fetch_sems.at[4]),
        pltpu.make_async_copy(echo_hbm, got.at[0], fetch_sems.at[5]),
        pltpu.make_async_copy(table_hbm, table_ref, fetch_sems.at[6]),
    ]
    barrier = pltpu.get_barrier_semaphore()
    for copy in fetches:
        copy.start()
    for d in range(1, groups):
        pl.semaphore_signal(
            barrier, inc=1, device_id={"pulse": lax.rem(group + d, groups)}, device_id_type=MESH
        )
    for d in range(1, n):
        pl.semaphore_signal(
            barrier, inc=1, device_id={"tile": lax.rem(tile + d, n)}, device_id_type=MESH
        )

    def names(strip, number):
        found = lists_ref[0, strip, 0] == number
        for j in range(1, lists_ref.shape[2]):
            found = found | (lists_ref[0, strip, j] == number)
        return found

    for copy in fetches[:2]:
        copy.wait()
    for b in range(held):
        for j, ref in enumerate((slope_ref, shift_ref)):
            for p in range(pulses):
                values[planes * b + pulses * j + p : planes * b + pulses * j + p + 1, :] = (
                    jnp.broadcast_to(ref[b : b + 1, p : p + 1].astype(F32), (1, 128))
                )
    pl.semaphore_wait(barrier, n - 1 + groups - 1)

    def remote(src, dst, send_sem, recv_sem, target):
        return pltpu.make_async_remote_copy(
            src_ref=src,
            dst_ref=dst,
            send_sem=send_sem,
            recv_sem=recv_sem,
            device_id=target,
            device_id_type=MESH,
        )

    infos = [
        remote(src, dst, info_sends.at[j], info_recvs.at[j], {"tile": far_tile})
        for j, (src, dst) in enumerate(
            ((starts_hbm, starts_far), (phase_hbm, phase_line.at[FAR]))
        )
    ]
    for copy in infos:
        copy.start()

    def block_copy(d):
        return remote(echo_hbm, got.at[d], sends.at[d], recvs.at[d], {"tile": partner(d)})

    def value_copy(d):
        return remote(
            values, got_values.at[d], value_sends.at[d], value_recvs.at[d], {"tile": partner(d)}
        )

    def send(d, c):
        block_copy(d).start()
        value_copy(d).start()
        return c

    lax.fori_loop(1, half, send, 0)

    lane = lax.broadcasted_iota(jnp.int32, (8, 128), 1)
    sub = lax.broadcasted_iota(jnp.int32, (8, 128), 0)
    wide[:, bins:, :] = jnp.zeros((planes, wide.shape[1] - bins, 128), F32)
    acc[...] = jnp.zeros_like(acc)
    strip_tile = (tile, far_tile)
    column_in_quad = (512 * sub + lane).astype(F32)

    def spread(strip):
        across = (rows, rows)
        diagonal = lax.broadcasted_iota(jnp.int32, across, 0) == lax.broadcasted_iota(
            jnp.int32, across, 1
        )
        line = jnp.where(diagonal, jnp.broadcast_to(phase_line[strip], across), 0.0)
        phase_ref[strip] = jnp.broadcast_to(jnp.sum(line, axis=1, keepdims=True), (rows, 128))

    def widen(strip, d):
        number = partner(d) * held
        block = got[d, 0]
        for b in range(1, held):
            block = jnp.where(names(strip_tile[strip], number + b), got[d, b], block)
        wide[:, :bins, :] = block.astype(F32).reshape(planes, bins, 128)

    def gather(strip, pair):
        for plane in range(planes):
            halves = []
            for h in range(2):
                row = 2 * pair + h
                begin = starts[strip, 0, row]
                at = begin // 128
                off = begin - 128 * at
                shift = lax.rem(128 - off, 128)
                keep = lane < 128 - off
                ys = [
                    pltpu.roll(wide[plane, pl.ds(at + o, 8, stride=3), :], shift, 1)
                    for o in range(5)
                ]
                halves.append([jnp.where(keep, ys[j], ys[j + 1]) for j in range(4)])
            for j in range(4):
                both = jnp.concatenate([halves[0][j], halves[1][j]], axis=0)
                lhs[plane, pl.ds(pl.multiple_of(16 * pair, 16), 16), 128 * j : 128 * j + 128] = (
                    both.astype(BF16)
                )

    def multiply():
        for plane in range(planes):
            product[plane, :, 0:256] = jnp.dot(
                lhs[plane, :, 0:256], table_ref[0:256, 0:256], preferred_element_type=F32
            )
            product[plane, :, 256:512] = jnp.dot(
                lhs[plane], table_ref[:, 256:512], preferred_element_type=F32
            )

    def phase(strip, d):
        number = partner(d) * held
        used = names(strip_tile[strip], number)
        tail = got_values[d, 0:planes]
        for b in range(1, held):
            named = names(strip_tile[strip], number + b)
            used = used | named
            tail = jnp.where(named, got_values[d, planes * b : planes * (b + 1)], tail)
        weight = jnp.where(used, 1.0, 0.0).astype(F32)
        for p in range(pulses):
            slope = tail[p : p + 1]
            shift = tail[pulses + p : pulses + p + 1]
            turn_im, turn_re = sine_cosine(phase_ref[strip] * shift)
            rowturn[p, 0] = turn_re
            rowturn[p, 1] = turn_im
            im, re = sine_cosine(column_in_quad * slope)
            step_im, step_re = sine_cosine(jnp.broadcast_to(128.0 * slope, (8, 128)))
            re = re * weight
            im = im * weight
            for q in range(4):
                ramp[p, 0, q] = re
                ramp[p, 1, q] = im
                re, im = re * step_re - im * step_im, re * step_im + im * step_re

    def acc_base(strip, plane):
        return (2 * strip + plane) * rows * KBLOCKS

    def turn(strip, pair):
        rows_at = [2 * pair, 2 * pair + 1]
        row_turn = [
            [[rowturn[p, part_of, pl.ds(r, 1), :] for part_of in range(2)] for p in range(pulses)]
            for r in rows_at
        ]
        for q in range(4):
            ramps = [[ramp[p, part_of, q] for part_of in range(2)] for p in range(pulses)]
            for h, r in enumerate(rows_at):
                at = pl.ds(pl.multiple_of(8 * r, 8), 8)
                at_re = pl.ds(pl.multiple_of(acc_base(strip, 0) + KBLOCKS * r + 8 * q, 8), 8)
                at_im = pl.ds(pl.multiple_of(acc_base(strip, 1) + KBLOCKS * r + 8 * q, 8), 8)
                total_re = acc[at_re, :]
                total_im = acc[at_im, :]
                for p in range(pulses):
                    row_re, row_im = row_turn[h][p]
                    ramp_re, ramp_im = ramps[p]
                    re = ramp_re * row_re - ramp_im * row_im
                    im = ramp_re * row_im + ramp_im * row_re
                    value_re = product[2 * p, at, 128 * q : 128 * q + 128]
                    value_im = product[2 * p + 1, at, 128 * q : 128 * q + 128]
                    total_re = total_re + (value_re * re - value_im * im)
                    total_im = total_im + (value_re * im + value_im * re)
                acc[at_re, :] = total_re
                acc[at_im, :] = total_im

    def rows_loop(gathered, turned):
        def step(pair, c):
            if gathered is not None:
                gather(gathered, pair)
            if turned is not None:
                turn(turned, pair)
            return c

        lax.fori_loop(0, rows // 2, step, 0, unroll=2)

    def arrive(d):
        value_copy(d).wait_recv()
        block_copy(d).wait_recv()

    def finish(strip, d):
        multiply()
        phase(strip, d)

    def part_copy(strip, d):
        target = lax.rem(group + d, groups)
        return remote(
            part.at[strip, target],
            got_part.at[strip, d - 1],
            part_sends.at[strip, d - 1],
            part_recvs.at[strip, d - 1],
            {"pulse": target},
        )

    wide_lane = lax.broadcasted_iota(jnp.int32, (rows, 128), 1)

    def column_block(strip, plane, k):
        start = acc_base(strip, plane) + QUADS * lax.rem(k, 4) + k // 4
        return acc[pl.ds(start, rows, stride=KBLOCKS), :] * scale

    def emit_strip(strip):
        def emit_for(g):
            for plane in range(2):
                for k in range(blocks):
                    if k < share:
                        value = column_block(strip, plane, share * g + k)
                    else:
                        value = jnp.where(
                            wide_lane < 64,
                            column_block(
                                strip, plane, jnp.minimum(share * (g + 1), KBLOCKS - 1)
                            ),
                            column_block(strip, plane, jnp.maximum(share * g - 1, 0)),
                        )
                    at = (plane * blocks + k) * rows
                    part[strip, g, at : at + rows, :] = value.astype(BF16)

        for d in range(groups - 1, 0, -1):
            emit_for(lax.rem(group + d, groups))
            part_copy(strip, d).start()
        emit_for(group)

    def summed(strip):
        for d in range(1, groups):
            part_copy(strip, d).wait_recv()
        total = part[strip, group].astype(F32)
        for d in range(1, groups):
            total = total + got_part[strip, d - 1].astype(F32)
        return total

    for copy in fetches[2:6]:
        copy.wait()
    spread(NEAR)
    got_values[0] = values[...]
    widen(NEAR, 0)
    rows_loop(NEAR, None)
    fetches[6].wait()
    finish(NEAR, 0)

    for copy in infos:
        copy.wait_recv()
    far_starts = pltpu.make_async_copy(starts_far, starts.at[FAR], fetch_sems.at[0])
    far_starts.start()
    spread(FAR)
    widen(FAR, 0)
    far_starts.wait()
    rows_loop(FAR, NEAR)
    finish(FAR, 0)

    def far_slot(d, c):
        arrive(d)
        widen(FAR, d)
        rows_loop(FAR, FAR)
        finish(FAR, d)
        return c

    lax.fori_loop(1, half, far_slot, 0)

    widen(NEAR, 1)
    rows_loop(NEAR, FAR)
    emit_strip(FAR)
    finish(NEAR, 1)

    def near_slot(d, c):
        widen(NEAR, d)
        rows_loop(NEAR, NEAR)
        finish(NEAR, d)
        return c

    lax.fori_loop(2, half, near_slot, 0)
    rows_loop(None, NEAR)
    emit_strip(NEAR)

    far_out[...] = summed(FAR).astype(BF16)
    cross = remote(far_out, far_in, far_sends.at[0], far_recvs.at[0], {"tile": far_tile})
    cross.start()
    total = summed(NEAR)
    cross.wait_recv()
    total = total + far_in[...].astype(F32)
    tall = rows + 16
    for i in range(2 * blocks):
        first[tall * i + 8 : tall * i + 8 + rows, :] = total[i * rows : (i + 1) * rows]
    for i in range(HALO):
        halo_out[1, i, 0 : 2 * blocks, :] = first[pl.ds(8 + i, 2 * blocks, stride=tall), :]
        halo_out[0, i, 0 : 2 * blocks, :] = first[
            pl.ds(8 + rows - HALO + i, 2 * blocks, stride=tall), :
        ]

    upward = remote(
        halo_out.at[1], halo.at[1], halo_sends.at[1], halo_recvs.at[1], {"tile": tile - 1}
    )
    downward = remote(
        halo_out.at[0], halo.at[0], halo_sends.at[0], halo_recvs.at[0], {"tile": tile + 1}
    )

    def put_halo(side, from_halo):
        for i in range(HALO):
            at = 8 - HALO + i if side == 0 else 8 + rows + i
            value = halo[side, i, 0 : 2 * blocks, :]
            if not from_halo:
                value = jnp.zeros_like(value)
            first[pl.ds(at, 2 * blocks, stride=tall), :] = value

    @pl.when(tile > 0)
    def _():
        upward.start()

    @pl.when(tile < n - 1)
    def _():
        downward.start()

    @pl.when(tile > 0)
    def _():
        downward.wait_recv()
        put_halo(0, True)

    @pl.when(tile == 0)
    def _():
        put_halo(0, False)

    @pl.when(tile < n - 1)
    def _():
        upward.wait_recv()
        put_halo(1, True)

    @pl.when(tile == n - 1)
    def _():
        put_halo(1, False)

    row = tile * rows - 8 + lax.broadcasted_iota(jnp.int32, (tall, 128), 0)
    line = lax.broadcasted_iota(jnp.int32, (1, 128), 1)
    tall_lane = lax.broadcasted_iota(jnp.int32, (tall, 128), 1)
    row_inside = (row >= 0) & (row < n * rows)
    row_down = (row >= 0) & (row < n * rows - 1)

    def sweep(source, write):
        field = [[source[tall * (p * blocks + k) : tall * (p * blocks + k + 1), :] for k in range(blocks)] for p in range(2)]
        down = [[], []]
        right = [[], []]
        for k in range(blocks):
            column = (group * share + k) * 128 + line
            if k == share:
                column = jnp.where(line < 64, column, column - 128 * blocks)
            column_inside = (column >= 0) & (column < NCOL)
            column_right = (column >= 0) & (column < NCOL - 1)
            square = floor_square
            for p in range(2):
                here = field[p][k]
                following = field[p][(k + 1) % blocks]
                beside = pltpu.roll(jnp.where(tall_lane == 0, following, here), 127, 1)
                below = pltpu.roll(here, tall - 1, 0)
                down[p].append(jnp.where(row_down & column_inside, below - here, 0.0))
                right[p].append(jnp.where(row_inside & column_right, beside - here, 0.0))
                square = square + (down[p][k] * down[p][k] + right[p][k] * right[p][k])
            inverse = lax.rsqrt(square)
            for p in range(2):
                down[p][k] = down[p][k] * inverse
                right[p][k] = right[p][k] * inverse
        for p in range(2):
            for k in range(blocks):
                before = right[p][(k - 1) % blocks]
                left = pltpu.roll(jnp.where(tall_lane == 127, before, right[p][k]), 1, 1)
                above = pltpu.roll(down[p][k], 1, 0)
                divergence = down[p][k] - above + right[p][k] - left
                at = tall * (p * blocks + k)
                here = field[p][k]
                base = first[at : at + tall, :]
                write(p, k, here - step_size * (here - base - tv_weight * divergence))

    def write_second(p, k, value):
        at = tall * (p * blocks + k)
        second[at : at + tall, :] = value

    def write_out(p, k, value):
        if k < share:
            out_ref[p, :, 128 * k : 128 * (k + 1)] = value[8 : 8 + rows]

    sweep(first, write_second)
    sweep(second, write_out)

    @pl.when(tile > 0)
    def _():
        upward.wait_send()

    @pl.when(tile < n - 1)
    def _():
        downward.wait_send()

    def sent(d, c):
        block_copy(d).wait_send()
        value_copy(d).wait_send()
        return c

    lax.fori_loop(1, half, sent, 0)
    for copy in infos:
        copy.wait_send()
    cross.wait_send()
    for strip in (NEAR, FAR):
        for d in range(1, groups):
            part_copy(strip, d).wait_send()


def body(echoes, pulse_slope, pulse_shift, footprint, band_start, row_phase):
    n = lax.axis_size("tile")
    groups = lax.axis_size("pulse")
    held, pulses = pulse_slope.shape
    rows = band_start.shape[0]
    bins = echoes.shape[3] // 128
    planes = 2 * pulses
    share = KBLOCKS // groups
    planes_of = echoes.reshape(held, planes * bins, 128)
    table = jnp.asarray(interpolation_table(), BF16)

    vmem = pl.BlockSpec(memory_space=pltpu.VMEM)
    anywhere = pl.BlockSpec(memory_space=pl.ANY)
    blocks = share + 1
    edge_rows = 8 * (-(-2 * blocks // 8))
    value_rows = 8 * (-(-held * planes // 8))
    field = (2 * blocks * (rows + 16), 128)
    piece = (2 * blocks * rows, 128)
    dma = pltpu.SemaphoreType.DMA
    refined = pl.pallas_call(
        functools.partial(kernel, held, pulses, rows, groups, n),
        out_shape=jax.ShapeDtypeStruct((2, rows, 128 * share), F32),
        in_specs=[anywhere] * 7,
        out_specs=vmem,
        scratch_shapes=[
            pltpu.SMEM(footprint.shape, jnp.int32),
            pltpu.VMEM((1, rows), jnp.int32),
            pltpu.SMEM((2, 1, rows), jnp.int32),
            pltpu.VMEM(pulse_slope.shape, BF16),
            pltpu.VMEM(pulse_shift.shape, BF16),
            pltpu.VMEM((2, 1, rows), F32),
            pltpu.VMEM((2, rows, 128), F32),
            pltpu.VMEM(table.shape, BF16),
            pltpu.VMEM((value_rows, 128), F32),
            pltpu.VMEM((n // 2, value_rows, 128), F32),
            pltpu.VMEM((n // 2,) + planes_of.shape, BF16),
            pltpu.VMEM((planes, bins + 8, 128), F32),
            pltpu.VMEM((planes, rows * QUADS, 512), BF16),
            pltpu.VMEM((planes, rows * QUADS, 512), F32),
            pltpu.VMEM((pulses, 2, 4, 8, 128), F32),
            pltpu.VMEM((pulses, 2, rows, 128), F32),
            pltpu.VMEM((4 * rows * KBLOCKS, 128), F32),
            pltpu.VMEM((2, groups) + piece, BF16),
            pltpu.VMEM((2, groups - 1) + piece, BF16),
            pltpu.VMEM(piece, BF16),
            pltpu.VMEM(piece, BF16),
            pltpu.VMEM(field, F32),
            pltpu.VMEM(field, F32),
            pltpu.VMEM((2, HALO, edge_rows, 128), F32),
            pltpu.VMEM((2, HALO, edge_rows, 128), F32),
            dma((7,)),
            dma((2,)),
            dma((2,)),
            dma((n // 2,)),
            dma((n // 2,)),
            dma((n // 2,)),
            dma((n // 2,)),
            dma((2, groups - 1)),
            dma((2, groups - 1)),
            dma((1,)),
            dma((1,)),
            dma((2,)),
            dma((2,)),
        ],
        compiler_params=pltpu.CompilerParams(
            collective_id=0, has_side_effects=True, vmem_limit_bytes=60 * 1024 * 1024
        ),
    )(
        footprint,
        band_start.reshape(1, rows),
        planes_of,
        pulse_slope,
        pulse_shift,
        row_phase.reshape(1, rows),
        table,
    )
    return refined


def solution(mesh):
    in_specs = (
        P(("pulse", "tile"), None, None, None),
        P(("pulse", "tile"), None),
        P(("pulse", "tile"), None),
        P("pulse", None, None),
        P("tile"),
        P("tile"),
    )
    out_specs = P(None, "tile", "pulse")
    return jax.shard_map(body, mesh=mesh, in_specs=in_specs, out_specs=out_specs, check_vma=False)
```

```python
import functools

import jax
import jax.numpy as jnp
import numpy as np
from jax import lax
from jax.experimental import pallas as pl
from jax.experimental.pallas import tpu as pltpu
from jax.sharding import PartitionSpec as P

NCOL = 4096
ITERS = 2
KBLOCKS = NCOL // 128
QUADS = KBLOCKS // 4
HALO = ITERS

step_size = 0.5
tv_weight = 0.4
floor_square = 0.25

MESH = pl.DeviceIdType.MESH
F32 = jnp.float32
BF16 = jnp.bfloat16


def interpolation_table():
    columns = np.arange(128)
    position = 3 * columns + 4
    base = position // 4
    f = (position % 4) / 4.0
    weights = [
        (-(f**3) + 2 * f**2 - f) / 2,
        (3 * f**3 - 5 * f**2 + 2) / 2,
        (-3 * f**3 + 4 * f**2 + f) / 2,
        (f**3 - f**2) / 2,
    ]
    table = np.zeros((512, 512), np.float32)
    for q in range(4):
        for shift, weight in zip(range(-1, 3), weights):
            table[96 * q + base + shift, 128 * q + columns] += weight
    return table


def sine_cosine(angle):
    turns = jnp.floor(angle * 0.6366197723675814 + 0.5)
    rest = angle - turns * 1.5703125
    rest = rest - turns * 4.837512969970703125e-4
    rest = rest - turns * 7.549789948768648e-8
    square = rest * rest
    sine = rest + rest * square * (
        -1.6666654611e-1 + square * (8.3321608736e-3 - square * 1.9515295891e-4)
    )
    cosine = (1.0 - 0.5 * square) + square * square * (
        4.166664568298827e-2 + square * (-1.388731625493765e-3 + square * 2.443315711809948e-5)
    )
    quarter = turns - 4.0 * jnp.floor(turns * 0.25)
    odd = (quarter == 1.0) | (quarter == 3.0)
    sine_sign = jnp.where(quarter >= 2.0, -1.0, 1.0)
    cosine_sign = jnp.where((quarter == 1.0) | (quarter == 2.0), -1.0, 1.0)
    return (
        sine_sign * jnp.where(odd, cosine, sine),
        cosine_sign * jnp.where(odd, sine, cosine),
    )


NEAR, FAR = 0, 1


def kernel(
    held,
    pulses,
    rows,
    groups,
    n,
    lists_hbm,
    starts_hbm,
    echo_hbm,
    slope_hbm,
    shift_hbm,
    phase_hbm,
    table_hbm,
    out_ref,
    lists_ref,
    starts_far,
    starts,
    slope_ref,
    shift_ref,
    phase_line,
    phase_ref,
    table_ref,
    values,
    got_values,
    got,
    wide,
    lhs,
    product,
    ramp,
    rowturn,
    acc,
    part,
    got_part,
    far_out,
    far_in,
    first,
    second,
    halo_out,
    halo,
    fetch_sems,
    info_sends,
    info_recvs,
    sends,
    recvs,
    value_sends,
    value_recvs,
    part_sends,
    part_recvs,
    far_sends,
    far_recvs,
    halo_sends,
    halo_recvs,
):
    planes = 2 * pulses
    bins = echo_hbm.shape[1] // planes
    share = KBLOCKS // groups
    blocks = share + 1
    scale = float(pulses * n * groups) ** -0.5
    group = lax.axis_index("pulse")
    tile = lax.axis_index("tile")
    half = n // 2
    far_tile = lax.rem(tile + half, n)
    local = lax.rem(tile, half)
    base_tile = tile - local
    power = half & (half - 1) == 0

    def partner(d):
        if not power:
            return base_tile + lax.rem(half + d - local, half)
        other = tile
        bit = 1
        while bit < half:
            other = other + ((d // bit) % 2) * bit * (1 - 2 * ((tile // bit) % 2))
            bit *= 2
        return other

    fetches = [
        pltpu.make_async_copy(slope_hbm, slope_ref, fetch_sems.at[0]),
        pltpu.make_async_copy(shift_hbm, shift_ref, fetch_sems.at[1]),
        pltpu.make_async_copy(starts_hbm, starts.at[NEAR], fetch_sems.at[2]),
        pltpu.make_async_copy(phase_hbm, phase_line.at[NEAR], fetch_sems.at[3]),
        pltpu.make_async_copy(lists_hbm, lists_ref, fetch_sems.at[4]),
        pltpu.make_async_copy(echo_hbm, got.at[0], fetch_sems.at[5]),
        pltpu.make_async_copy(table_hbm, table_ref, fetch_sems.at[6]),
    ]
    barrier = pltpu.get_barrier_semaphore()
    for copy in fetches:
        copy.start()
    for d in range(1, groups):
        pl.semaphore_signal(
            barrier, inc=1, device_id={"pulse": lax.rem(group + d, groups)}, device_id_type=MESH
        )
    for d in range(1, n):
        pl.semaphore_signal(
            barrier, inc=1, device_id={"tile": lax.rem(tile + d, n)}, device_id_type=MESH
        )

    def names(strip, number):
        found = lists_ref[0, strip, 0] == number
        for j in range(1, lists_ref.shape[2]):
            found = found | (lists_ref[0, strip, j] == number)
        return found

    for copy in fetches[:2]:
        copy.wait()
    for b in range(held):
        for j, ref in enumerate((slope_ref, shift_ref)):
            for p in range(pulses):
                values[planes * b + pulses * j + p : planes * b + pulses * j + p + 1, :] = (
                    jnp.broadcast_to(ref[b : b + 1, p : p + 1].astype(F32), (1, 128))
                )
    pl.semaphore_wait(barrier, n - 1 + groups - 1)

    def remote(src, dst, send_sem, recv_sem, target):
        return pltpu.make_async_remote_copy(
            src_ref=src,
            dst_ref=dst,
            send_sem=send_sem,
            recv_sem=recv_sem,
            device_id=target,
            device_id_type=MESH,
        )

    infos = [
        remote(src, dst, info_sends.at[j], info_recvs.at[j], {"tile": far_tile})
        for j, (src, dst) in enumerate(
            ((starts_hbm, starts_far), (phase_hbm, phase_line.at[FAR]))
        )
    ]
    for copy in infos:
        copy.start()

    def block_copy(d):
        return remote(echo_hbm, got.at[d], sends.at[d], recvs.at[d], {"tile": partner(d)})

    def value_copy(d):
        return remote(
            values, got_values.at[d], value_sends.at[d], value_recvs.at[d], {"tile": partner(d)}
        )

    def send(d, c):
        block_copy(d).start()
        value_copy(d).start()
        return c

    lax.fori_loop(1, half, send, 0)

    lane = lax.broadcasted_iota(jnp.int32, (8, 128), 1)
    sub = lax.broadcasted_iota(jnp.int32, (8, 128), 0)
    wide[:, bins:, :] = jnp.zeros((planes, wide.shape[1] - bins, 128), F32)
    for ref in (acc, lhs, product, ramp, rowturn):
        ref[...] = jnp.zeros_like(ref)
    column_in_quad = (512 * sub + lane).astype(F32)

    def tile_of(strip):
        return jnp.where(strip == FAR, far_tile, tile)

    def spread(strip):
        across = (rows, rows)
        diagonal = lax.broadcasted_iota(jnp.int32, across, 0) == lax.broadcasted_iota(
            jnp.int32, across, 1
        )
        line = jnp.where(diagonal, jnp.broadcast_to(phase_line[strip], across), 0.0)
        phase_ref[strip] = jnp.broadcast_to(jnp.sum(line, axis=1, keepdims=True), (rows, 128))

    def widen(strip, d):
        number = partner(d) * held
        block = got[d, 0]
        for b in range(1, held):
            block = jnp.where(names(tile_of(strip), number + b), got[d, b], block)
        wide[:, :bins, :] = block.astype(F32).reshape(planes, bins, 128)

    def gather(strip, chunk):
        side = chunk % 2
        for pair in range(4):
            for plane in range(planes):
                halves = []
                for h in range(2):
                    begin = starts[strip, 0, 8 * chunk + 2 * pair + h]
                    at = begin // 128
                    off = begin - 128 * at
                    shift = lax.rem(128 - off, 128)
                    keep = lane < 128 - off
                    ys = [
                        pltpu.roll(wide[plane, pl.ds(at + o, 8, stride=3), :], shift, 1)
                        for o in range(5)
                    ]
                    halves.append([jnp.where(keep, ys[j], ys[j + 1]) for j in range(4)])
                for j in range(4):
                    both = jnp.concatenate([halves[0][j], halves[1][j]], axis=0)
                    at_row = 64 * plane + 16 * pair
                    lhs[side, at_row : at_row + 16, 128 * j : 128 * j + 128] = both.astype(BF16)

    def multiply(chunk):
        side = chunk % 2
        product[side, :, 0:256] = jnp.dot(
            lhs[side, :, 0:256], table_ref[0:256, 0:256], preferred_element_type=F32
        )
        product[side, :, 256:512] = jnp.dot(
            lhs[side], table_ref[:, 256:512], preferred_element_type=F32
        )

    def phase(strip, d):
        number = partner(d) * held
        used = names(tile_of(strip), number)
        tail = got_values[d, 0:planes]
        for b in range(1, held):
            named = names(tile_of(strip), number + b)
            used = used | named
            tail = jnp.where(named, got_values[d, planes * b : planes * (b + 1)], tail)
        weight = jnp.where(used, 1.0, 0.0).astype(F32)
        for p in range(pulses):
            slope = tail[p : p + 1]
            shift = tail[pulses + p : pulses + p + 1]
            turn_im, turn_re = sine_cosine(phase_ref[strip] * shift)
            rowturn[p, 0] = turn_re
            rowturn[p, 1] = turn_im
            im, re = sine_cosine(column_in_quad * slope)
            step_im, step_re = sine_cosine(jnp.broadcast_to(128.0 * slope, (8, 128)))
            re = re * weight
            im = im * weight
            for q in range(4):
                ramp[p, 0, q] = re
                ramp[p, 1, q] = im
                re, im = re * step_re - im * step_im, re * step_im + im * step_re

    def acc_base(strip, plane):
        return (2 * strip + plane) * rows * KBLOCKS

    def turn(strip, chunk):
        side = chunk % 2
        row_turn = [
            [
                [rowturn[p, part_of, 8 * chunk + r : 8 * chunk + r + 1, :] for part_of in range(2)]
                for p in range(pulses)
            ]
            for r in range(8)
        ]
        for q in range(4):
            ramps = [[ramp[p, part_of, q] for part_of in range(2)] for p in range(pulses)]
            for r in range(8):
                at_row = KBLOCKS * (8 * chunk + r) + 8 * q
                at_re = pl.ds(pl.multiple_of(acc_base(strip, 0) + at_row, 8), 8)
                at_im = pl.ds(pl.multiple_of(acc_base(strip, 1) + at_row, 8), 8)
                total_re = acc[at_re, :]
                total_im = acc[at_im, :]
                for p in range(pulses):
                    row_re, row_im = row_turn[r][p]
                    ramp_re, ramp_im = ramps[p]
                    re = ramp_re * row_re - ramp_im * row_im
                    im = ramp_re * row_im + ramp_im * row_re
                    at = 128 * p + 8 * r
                    value_re = product[side, at : at + 8, 128 * q : 128 * q + 128]
                    value_im = product[side, at + 64 : at + 72, 128 * q : 128 * q + 128]
                    total_re = total_re + (value_re * re - value_im * im)
                    total_im = total_im + (value_re * im + value_im * re)
                acc[at_re, :] = total_re
                acc[at_im, :] = total_im

    def arrive(d):
        value_copy(d).wait_recv()
        block_copy(d).wait_recv()

    def part_copy(strip, d):
        target = lax.rem(group + d, groups)
        return remote(
            part.at[strip, target],
            got_part.at[strip, d - 1],
            part_sends.at[strip, d - 1],
            part_recvs.at[strip, d - 1],
            {"pulse": target},
        )

    wide_lane = lax.broadcasted_iota(jnp.int32, (rows, 128), 1)

    def column_block(strip, plane, k):
        start = acc_base(strip, plane) + QUADS * lax.rem(k, 4) + k // 4
        return acc[pl.ds(start, rows, stride=KBLOCKS), :] * scale

    def emit_strip(strip):
        def emit_for(g):
            for plane in range(2):
                for k in range(blocks):
                    if k < share:
                        value = column_block(strip, plane, share * g + k)
                    else:
                        value = jnp.where(
                            wide_lane < 64,
                            column_block(
                                strip, plane, jnp.minimum(share * (g + 1), KBLOCKS - 1)
                            ),
                            column_block(strip, plane, jnp.maximum(share * g - 1, 0)),
                        )
                    at = (plane * blocks + k) * rows
                    part[strip, g, at : at + rows, :] = value.astype(BF16)

        for d in range(groups - 1, 0, -1):
            emit_for(lax.rem(group + d, groups))
            part_copy(strip, d).start()
        emit_for(group)

    def summed(strip):
        for d in range(1, groups):
            part_copy(strip, d).wait_recv()
        total = part[strip, group].astype(F32)
        for d in range(1, groups):
            total = total + got_part[strip, d - 1].astype(F32)
        return total

    for copy in fetches[2:6]:
        copy.wait()
    spread(NEAR)
    got_values[0] = values[...]
    fetches[6].wait()
    chunks = rows // 8
    far_starts = pltpu.make_async_copy(starts_far, starts.at[FAR], fetch_sems.at[0])

    def place_of(i):
        far = (i >= 1) & (i <= half)
        d = jnp.where(far, i - 1, jnp.where(i > half, i - half, 0))
        return jnp.where(far, FAR, NEAR), d

    def slot(i, c):
        strip, d = place_of(i)
        last_strip, _ = place_of(i - 1)

        @pl.when(i == 1)
        def _():
            for copy in infos:
                copy.wait_recv()
            far_starts.start()
            spread(FAR)
            far_starts.wait()

        @pl.when((i >= 2) & (i <= half))
        def _():
            arrive(d)

        widen(strip, d)
        for chunk in range(chunks):
            gather(strip, chunk)
            multiply((chunk - 1) % chunks)
            if chunk < 2:
                turn(last_strip, (chunk - 2) % chunks)
            else:
                turn(strip, chunk - 2)
            if chunk == 1:
                phase(strip, d)
        return c

    lax.fori_loop(0, half + 2, slot, 0)
    emit_strip(FAR)
    lax.fori_loop(half + 2, n, slot, 0)
    multiply(chunks - 1)
    turn(NEAR, chunks - 2)
    turn(NEAR, chunks - 1)
    emit_strip(NEAR)

    far_out[...] = summed(FAR).astype(BF16)
    cross = remote(far_out, far_in, far_sends.at[0], far_recvs.at[0], {"tile": far_tile})
    cross.start()
    total = summed(NEAR)
    cross.wait_recv()
    total = total + far_in[...].astype(F32)
    tall = rows + 16
    for i in range(2 * blocks):
        first[tall * i + 8 : tall * i + 8 + rows, :] = total[i * rows : (i + 1) * rows]
    for i in range(HALO):
        halo_out[1, i, 0 : 2 * blocks, :] = first[pl.ds(8 + i, 2 * blocks, stride=tall), :]
        halo_out[0, i, 0 : 2 * blocks, :] = first[
            pl.ds(8 + rows - HALO + i, 2 * blocks, stride=tall), :
        ]

    upward = remote(
        halo_out.at[1], halo.at[1], halo_sends.at[1], halo_recvs.at[1], {"tile": tile - 1}
    )
    downward = remote(
        halo_out.at[0], halo.at[0], halo_sends.at[0], halo_recvs.at[0], {"tile": tile + 1}
    )

    def put_halo(side, from_halo):
        for i in range(HALO):
            at = 8 - HALO + i if side == 0 else 8 + rows + i
            value = halo[side, i, 0 : 2 * blocks, :]
            if not from_halo:
                value = jnp.zeros_like(value)
            first[pl.ds(at, 2 * blocks, stride=tall), :] = value

    @pl.when(tile > 0)
    def _():
        upward.start()

    @pl.when(tile < n - 1)
    def _():
        downward.start()

    @pl.when(tile > 0)
    def _():
        downward.wait_recv()
        put_halo(0, True)

    @pl.when(tile == 0)
    def _():
        put_halo(0, False)

    @pl.when(tile < n - 1)
    def _():
        upward.wait_recv()
        put_halo(1, True)

    @pl.when(tile == n - 1)
    def _():
        put_halo(1, False)

    row = tile * rows - 8 + lax.broadcasted_iota(jnp.int32, (tall, 128), 0)
    line = lax.broadcasted_iota(jnp.int32, (1, 128), 1)
    tall_lane = lax.broadcasted_iota(jnp.int32, (tall, 128), 1)
    row_inside = (row >= 0) & (row < n * rows)
    row_down = (row >= 0) & (row < n * rows - 1)

    def sweep(source, write):
        field = [[source[tall * (p * blocks + k) : tall * (p * blocks + k + 1), :] for k in range(blocks)] for p in range(2)]
        down = [[], []]
        right = [[], []]
        for k in range(blocks):
            column = (group * share + k) * 128 + line
            if k == share:
                column = jnp.where(line < 64, column, column - 128 * blocks)
            column_inside = (column >= 0) & (column < NCOL)
            column_right = (column >= 0) & (column < NCOL - 1)
            square = floor_square
            for p in range(2):
                here = field[p][k]
                following = field[p][(k + 1) % blocks]
                beside = pltpu.roll(jnp.where(tall_lane == 0, following, here), 127, 1)
                below = pltpu.roll(here, tall - 1, 0)
                down[p].append(jnp.where(row_down & column_inside, below - here, 0.0))
                right[p].append(jnp.where(row_inside & column_right, beside - here, 0.0))
                square = square + (down[p][k] * down[p][k] + right[p][k] * right[p][k])
            inverse = lax.rsqrt(square)
            for p in range(2):
                down[p][k] = down[p][k] * inverse
                right[p][k] = right[p][k] * inverse
        for p in range(2):
            for k in range(blocks):
                before = right[p][(k - 1) % blocks]
                left = pltpu.roll(jnp.where(tall_lane == 127, before, right[p][k]), 1, 1)
                above = pltpu.roll(down[p][k], 1, 0)
                divergence = down[p][k] - above + right[p][k] - left
                at = tall * (p * blocks + k)
                here = field[p][k]
                base = first[at : at + tall, :]
                write(p, k, here - step_size * (here - base - tv_weight * divergence))

    def write_second(p, k, value):
        at = tall * (p * blocks + k)
        second[at : at + tall, :] = value

    def write_out(p, k, value):
        if k < share:
            out_ref[p, :, 128 * k : 128 * (k + 1)] = value[8 : 8 + rows]

    sweep(first, write_second)
    sweep(second, write_out)

    @pl.when(tile > 0)
    def _():
        upward.wait_send()

    @pl.when(tile < n - 1)
    def _():
        downward.wait_send()

    def sent(d, c):
        block_copy(d).wait_send()
        value_copy(d).wait_send()
        return c

    lax.fori_loop(1, half, sent, 0)
    for copy in infos:
        copy.wait_send()
    cross.wait_send()
    for strip in (NEAR, FAR):
        for d in range(1, groups):
            part_copy(strip, d).wait_send()


def body(echoes, pulse_slope, pulse_shift, footprint, band_start, row_phase):
    n = lax.axis_size("tile")
    groups = lax.axis_size("pulse")
    held, pulses = pulse_slope.shape
    rows = band_start.shape[0]
    bins = echoes.shape[3] // 128
    planes = 2 * pulses
    share = KBLOCKS // groups
    planes_of = echoes.reshape(held, planes * bins, 128)
    table = jnp.asarray(interpolation_table(), BF16)

    vmem = pl.BlockSpec(memory_space=pltpu.VMEM)
    anywhere = pl.BlockSpec(memory_space=pl.ANY)
    blocks = share + 1
    edge_rows = 8 * (-(-2 * blocks // 8))
    value_rows = 8 * (-(-held * planes // 8))
    field = (2 * blocks * (rows + 16), 128)
    piece = (2 * blocks * rows, 128)
    dma = pltpu.SemaphoreType.DMA
    refined = pl.pallas_call(
        functools.partial(kernel, held, pulses, rows, groups, n),
        out_shape=jax.ShapeDtypeStruct((2, rows, 128 * share), F32),
        in_specs=[anywhere] * 7,
        out_specs=vmem,
        scratch_shapes=[
            pltpu.SMEM(footprint.shape, jnp.int32),
            pltpu.VMEM((1, rows), jnp.int32),
            pltpu.SMEM((2, 1, rows), jnp.int32),
            pltpu.VMEM(pulse_slope.shape, BF16),
            pltpu.VMEM(pulse_shift.shape, BF16),
            pltpu.VMEM((2, 1, rows), F32),
            pltpu.VMEM((2, rows, 128), F32),
            pltpu.VMEM(table.shape, BF16),
            pltpu.VMEM((value_rows, 128), F32),
            pltpu.VMEM((n // 2, value_rows, 128), F32),
            pltpu.VMEM((n // 2,) + planes_of.shape, BF16),
            pltpu.VMEM((planes, bins + 8, 128), F32),
            pltpu.VMEM((2, planes * 64, 512), BF16),
            pltpu.VMEM((2, planes * 64, 512), F32),
            pltpu.VMEM((pulses, 2, 4, 8, 128), F32),
            pltpu.VMEM((pulses, 2, rows, 128), F32),
            pltpu.VMEM((4 * rows * KBLOCKS, 128), F32),
            pltpu.VMEM((2, groups) + piece, BF16),
            pltpu.VMEM((2, groups - 1) + piece, BF16),
            pltpu.VMEM(piece, BF16),
            pltpu.VMEM(piece, BF16),
            pltpu.VMEM(field, F32),
            pltpu.VMEM(field, F32),
            pltpu.VMEM((2, HALO, edge_rows, 128), F32),
            pltpu.VMEM((2, HALO, edge_rows, 128), F32),
            dma((7,)),
            dma((2,)),
            dma((2,)),
            dma((n // 2,)),
            dma((n // 2,)),
            dma((n // 2,)),
            dma((n // 2,)),
            dma((2, groups - 1)),
            dma((2, groups - 1)),
            dma((1,)),
            dma((1,)),
            dma((2,)),
            dma((2,)),
        ],
        compiler_params=pltpu.CompilerParams(
            collective_id=0, has_side_effects=True, vmem_limit_bytes=60 * 1024 * 1024
        ),
    )(
        footprint,
        band_start.reshape(1, rows),
        planes_of,
        pulse_slope,
        pulse_shift,
        row_phase.reshape(1, rows),
        table,
    )
    return refined


def solution(mesh):
    in_specs = (
        P(("pulse", "tile"), None, None, None),
        P(("pulse", "tile"), None),
        P(("pulse", "tile"), None),
        P("pulse", None, None),
        P("tile"),
        P("tile"),
    )
    out_specs = P(None, "tile", "pulse")
    return jax.shard_map(body, mesh=mesh, in_specs=in_specs, out_specs=out_specs, check_vma=False)
```

```python
import functools

import jax
import jax.numpy as jnp
import numpy as np
from jax import lax
from jax.experimental import pallas as pl
from jax.experimental.pallas import tpu as pltpu
from jax.sharding import PartitionSpec as P

NCOL = 4096
ITERS = 2
KBLOCKS = NCOL // 128
QUADS = KBLOCKS // 4
HALO = ITERS

step_size = 0.5
tv_weight = 0.4
floor_square = 0.25

MESH = pl.DeviceIdType.MESH
F32 = jnp.float32
BF16 = jnp.bfloat16


def interpolation_table():
    columns = np.arange(128)
    position = 3 * columns + 4
    base = position // 4
    f = (position % 4) / 4.0
    weights = [
        (-(f**3) + 2 * f**2 - f) / 2,
        (3 * f**3 - 5 * f**2 + 2) / 2,
        (-3 * f**3 + 4 * f**2 + f) / 2,
        (f**3 - f**2) / 2,
    ]
    table = np.zeros((512, 512), np.float32)
    for q in range(4):
        for shift, weight in zip(range(-1, 3), weights):
            table[96 * q + base + shift, 128 * q + columns] += weight
    return table


def sine_cosine(angle):
    turns = jnp.floor(angle * 0.6366197723675814 + 0.5)
    rest = angle - turns * 1.5703125
    rest = rest - turns * 4.837512969970703125e-4
    rest = rest - turns * 7.549789948768648e-8
    square = rest * rest
    sine = rest + rest * square * (
        -1.6666654611e-1 + square * (8.3321608736e-3 - square * 1.9515295891e-4)
    )
    cosine = (1.0 - 0.5 * square) + square * square * (
        4.166664568298827e-2 + square * (-1.388731625493765e-3 + square * 2.443315711809948e-5)
    )
    quarter = turns - 4.0 * jnp.floor(turns * 0.25)
    odd = (quarter == 1.0) | (quarter == 3.0)
    sine_sign = jnp.where(quarter >= 2.0, -1.0, 1.0)
    cosine_sign = jnp.where((quarter == 1.0) | (quarter == 2.0), -1.0, 1.0)
    return (
        sine_sign * jnp.where(odd, cosine, sine),
        cosine_sign * jnp.where(odd, sine, cosine),
    )


NEAR, FAR = 0, 1


def kernel(
    held,
    pulses,
    rows,
    groups,
    n,
    lists_hbm,
    starts_hbm,
    echo_hbm,
    slope_hbm,
    shift_hbm,
    phase_hbm,
    table_hbm,
    out_ref,
    lists_ref,
    starts_far,
    starts,
    slope_ref,
    shift_ref,
    phase_line,
    phase_ref,
    table_ref,
    values,
    got_values,
    got,
    wide,
    lhs,
    product,
    ramp,
    rowturn,
    acc,
    part,
    got_part,
    far_out,
    far_in,
    first,
    second,
    halo_out,
    halo,
    fetch_sems,
    info_sends,
    info_recvs,
    sends,
    recvs,
    value_sends,
    value_recvs,
    part_sends,
    part_recvs,
    far_sends,
    far_recvs,
    halo_sends,
    halo_recvs,
):
    planes = 2 * pulses
    bins = echo_hbm.shape[1] // planes
    share = KBLOCKS // groups
    blocks = share + 1
    scale = float(pulses * n * groups) ** -0.5
    group = lax.axis_index("pulse")
    tile = lax.axis_index("tile")
    half = n // 2
    far_tile = lax.rem(tile + half, n)
    local = lax.rem(tile, half)
    base_tile = tile - local
    power = half & (half - 1) == 0

    def partner(d):
        if not power:
            return base_tile + lax.rem(half + d - local, half)
        other = tile
        bit = 1
        while bit < half:
            other = other + ((d // bit) % 2) * bit * (1 - 2 * ((tile // bit) % 2))
            bit *= 2
        return other

    fetches = [
        pltpu.make_async_copy(slope_hbm, slope_ref, fetch_sems.at[0]),
        pltpu.make_async_copy(shift_hbm, shift_ref, fetch_sems.at[1]),
        pltpu.make_async_copy(starts_hbm, starts.at[NEAR], fetch_sems.at[2]),
        pltpu.make_async_copy(phase_hbm, phase_line.at[NEAR], fetch_sems.at[3]),
        pltpu.make_async_copy(lists_hbm, lists_ref, fetch_sems.at[4]),
        pltpu.make_async_copy(echo_hbm, got.at[0], fetch_sems.at[5]),
        pltpu.make_async_copy(table_hbm, table_ref, fetch_sems.at[6]),
    ]
    barrier = pltpu.get_barrier_semaphore()
    for copy in fetches:
        copy.start()
    for d in range(1, groups):
        pl.semaphore_signal(
            barrier, inc=1, device_id={"pulse": lax.rem(group + d, groups)}, device_id_type=MESH
        )
    for d in range(1, n):
        pl.semaphore_signal(
            barrier, inc=1, device_id={"tile": lax.rem(tile + d, n)}, device_id_type=MESH
        )

    def names(strip, number):
        found = lists_ref[0, strip, 0] == number
        for j in range(1, lists_ref.shape[2]):
            found = found | (lists_ref[0, strip, j] == number)
        return found

    for copy in fetches[:2]:
        copy.wait()
    for b in range(held):
        for j, ref in enumerate((slope_ref, shift_ref)):
            for p in range(pulses):
                values[planes * b + pulses * j + p : planes * b + pulses * j + p + 1, :] = (
                    jnp.broadcast_to(ref[b : b + 1, p : p + 1].astype(F32), (1, 128))
                )
    pl.semaphore_wait(barrier, n - 1 + groups - 1)

    def remote(src, dst, send_sem, recv_sem, target):
        return pltpu.make_async_remote_copy(
            src_ref=src,
            dst_ref=dst,
            send_sem=send_sem,
            recv_sem=recv_sem,
            device_id=target,
            device_id_type=MESH,
        )

    infos = [
        remote(src, dst, info_sends.at[j], info_recvs.at[j], {"tile": far_tile})
        for j, (src, dst) in enumerate(
            ((starts_hbm, starts_far), (phase_hbm, phase_line.at[FAR]))
        )
    ]
    for copy in infos:
        copy.start()

    def block_copy(d):
        return remote(echo_hbm, got.at[d], sends.at[d], recvs.at[d], {"tile": partner(d)})

    def value_copy(d):
        return remote(
            values, got_values.at[d], value_sends.at[d], value_recvs.at[d], {"tile": partner(d)}
        )

    def send(d, c):
        block_copy(d).start()
        value_copy(d).start()
        return c

    lax.fori_loop(1, half, send, 0)

    lane = lax.broadcasted_iota(jnp.int32, (8, 128), 1)
    sub = lax.broadcasted_iota(jnp.int32, (8, 128), 0)
    wide[:, bins:, :] = jnp.zeros((planes, wide.shape[1] - bins, 128), F32)
    for ref in (acc, lhs, product, ramp, rowturn):
        ref[...] = jnp.zeros_like(ref)
    column_in_quad = (512 * sub + lane).astype(F32)

    def tile_of(strip):
        return jnp.where(strip == FAR, far_tile, tile)

    def spread(strip):
        across = (rows, rows)
        diagonal = lax.broadcasted_iota(jnp.int32, across, 0) == lax.broadcasted_iota(
            jnp.int32, across, 1
        )
        line = jnp.where(diagonal, jnp.broadcast_to(phase_line[strip], across), 0.0)
        phase_ref[strip] = jnp.broadcast_to(jnp.sum(line, axis=1, keepdims=True), (rows, 128))

    def widen(strip, d):
        number = partner(d) * held
        block = got[d, 0]
        for b in range(1, held):
            block = jnp.where(names(tile_of(strip), number + b), got[d, b], block)
        wide[:, :bins, :] = block.astype(F32).reshape(planes, bins, 128)

    def gather(strip, chunk):
        side = chunk % 2
        for pair in range(4):
            for plane in range(planes):
                halves = []
                for h in range(2):
                    begin = starts[strip, 0, 8 * chunk + 2 * pair + h]
                    at = begin // 128
                    off = begin - 128 * at
                    shift = lax.rem(128 - off, 128)
                    keep = lane < 128 - off
                    ys = [
                        pltpu.roll(wide[plane, pl.ds(at + o, 8, stride=3), :], shift, 1)
                        for o in range(5)
                    ]
                    halves.append([jnp.where(keep, ys[j], ys[j + 1]) for j in range(4)])
                for j in range(4):
                    both = jnp.concatenate([halves[0][j], halves[1][j]], axis=0)
                    at_row = 64 * plane + 16 * pair
                    lhs[side, at_row : at_row + 16, 128 * j : 128 * j + 128] = both.astype(BF16)

    def multiply(chunk):
        side = chunk % 2
        product[side, :, 0:256] = jnp.dot(
            lhs[side, :, 0:256], table_ref[0:256, 0:256], preferred_element_type=F32
        )
        product[side, :, 256:512] = jnp.dot(
            lhs[side], table_ref[:, 256:512], preferred_element_type=F32
        )

    def phase(strip, d):
        number = partner(d) * held
        used = names(tile_of(strip), number)
        tail = got_values[d, 0:planes]
        for b in range(1, held):
            named = names(tile_of(strip), number + b)
            used = used | named
            tail = jnp.where(named, got_values[d, planes * b : planes * (b + 1)], tail)
        weight = jnp.where(used, 1.0, 0.0).astype(F32)
        for p in range(pulses):
            slope = tail[p : p + 1]
            shift = tail[pulses + p : pulses + p + 1]
            turn_im, turn_re = sine_cosine(phase_ref[strip] * shift)
            rowturn[p, 0] = turn_re
            rowturn[p, 1] = turn_im
            im, re = sine_cosine(column_in_quad * slope)
            step_im, step_re = sine_cosine(jnp.broadcast_to(128.0 * slope, (8, 128)))
            re = re * weight
            im = im * weight
            for q in range(4):
                ramp[p, 0, q] = re
                ramp[p, 1, q] = im
                re, im = re * step_re - im * step_im, re * step_im + im * step_re

    def acc_base(strip, plane):
        return (2 * strip + plane) * rows * KBLOCKS

    def turn(strip, chunk):
        side = chunk % 2
        row_turn = [
            [
                [rowturn[p, part_of, 8 * chunk + r : 8 * chunk + r + 1, :] for part_of in range(2)]
                for p in range(pulses)
            ]
            for r in range(8)
        ]
        for q in range(4):
            ramps = [[ramp[p, part_of, q] for part_of in range(2)] for p in range(pulses)]
            for r in range(8):
                at_row = KBLOCKS * (8 * chunk + r) + 8 * q
                at_re = pl.ds(pl.multiple_of(acc_base(strip, 0) + at_row, 8), 8)
                at_im = pl.ds(pl.multiple_of(acc_base(strip, 1) + at_row, 8), 8)
                total_re = acc[at_re, :]
                total_im = acc[at_im, :]
                for p in range(pulses):
                    row_re, row_im = row_turn[r][p]
                    ramp_re, ramp_im = ramps[p]
                    re = ramp_re * row_re - ramp_im * row_im
                    im = ramp_re * row_im + ramp_im * row_re
                    at = 128 * p + 8 * r
                    value_re = product[side, at : at + 8, 128 * q : 128 * q + 128]
                    value_im = product[side, at + 64 : at + 72, 128 * q : 128 * q + 128]
                    total_re = total_re + (value_re * re - value_im * im)
                    total_im = total_im + (value_re * im + value_im * re)
                acc[at_re, :] = total_re
                acc[at_im, :] = total_im

    def arrive(d):
        value_copy(d).wait_recv()
        block_copy(d).wait_recv()

    half_rows = rows // 2

    def part_copy(strip, d, side):
        target = lax.rem(group + d, groups)
        return remote(
            part.at[strip, target, side],
            got_part.at[strip, d - 1, side],
            part_sends.at[strip, d - 1, side],
            part_recvs.at[strip, d - 1, side],
            {"pulse": target},
        )

    wide_lane = lax.broadcasted_iota(jnp.int32, (half_rows, 128), 1)

    def emit_for(strip, side, g):
        def column_block(plane, k):
            start = acc_base(strip, plane) + side * half_rows * KBLOCKS
            start = start + QUADS * lax.rem(k, 4) + k // 4
            return acc[pl.ds(start, half_rows, stride=KBLOCKS), :] * scale

        for plane in range(2):
            for k in range(blocks):
                if k < share:
                    value = column_block(plane, share * g + k)
                else:
                    value = jnp.where(
                        wide_lane < 64,
                        column_block(plane, jnp.minimum(share * (g + 1), KBLOCKS - 1)),
                        column_block(plane, jnp.maximum(share * g - 1, 0)),
                    )
                at = (plane * blocks + k) * half_rows
                part[strip, g, side, at : at + half_rows, :] = value.astype(BF16)

    def emit_and_send(strip, side):
        for d in range(groups - 1, 0, -1):
            emit_for(strip, side, lax.rem(group + d, groups))
            part_copy(strip, d, side).start()

    def summed(strip, side):
        for d in range(1, groups):
            part_copy(strip, d, side).wait_recv()
        total = part[strip, group, side].astype(F32)
        for d in range(1, groups):
            total = total + got_part[strip, d - 1, side].astype(F32)
        return total

    for copy in fetches[2:6]:
        copy.wait()
    spread(NEAR)
    got_values[0] = values[...]
    fetches[6].wait()
    chunks = rows // 8
    far_starts = pltpu.make_async_copy(starts_far, starts.at[FAR], fetch_sems.at[0])

    def place_of(i):
        far = (i >= 1) & (i <= half)
        d = jnp.where(far, i - 1, jnp.where(i > half, i - half, 0))
        return jnp.where(far, FAR, NEAR), d

    def slot(i, c):
        strip, d = place_of(i)
        last_strip, _ = place_of(i - 1)

        @pl.when(i == 1)
        def _():
            for copy in infos:
                copy.wait_recv()
            far_starts.start()
            spread(FAR)
            far_starts.wait()

        @pl.when((i >= 2) & (i <= half))
        def _():
            arrive(d)

        widen(strip, d)
        for chunk in range(chunks):
            gather(strip, chunk)
            multiply((chunk - 1) % chunks)
            if chunk < 2:
                turn(last_strip, (chunk - 2) % chunks)
            else:
                turn(strip, chunk - 2)
            if chunk == 1:
                phase(strip, d)
        return c

    lax.fori_loop(0, half + 2, slot, 0)
    for side in range(2):
        emit_and_send(FAR, side)
        emit_for(FAR, side, group)
    lax.fori_loop(half + 2, n, slot, 0)
    emit_and_send(NEAR, 0)
    multiply(chunks - 1)
    turn(NEAR, chunks - 2)
    turn(NEAR, chunks - 1)
    emit_and_send(NEAR, 1)

    for side in range(2):
        far_out[side] = summed(FAR, side).astype(BF16)
    cross = remote(far_out, far_in, far_sends.at[0], far_recvs.at[0], {"tile": far_tile})
    cross.start()
    for side in range(2):
        emit_for(NEAR, side, group)
    totals = [summed(NEAR, side) for side in range(2)]
    cross.wait_recv()
    totals = [totals[side] + far_in[side].astype(F32) for side in range(2)]
    tall = rows + 16
    for i in range(2 * blocks):
        for side in range(2):
            at = tall * i + 8 + side * half_rows
            first[at : at + half_rows, :] = totals[side][i * half_rows : (i + 1) * half_rows]
    for i in range(HALO):
        halo_out[1, i, 0 : 2 * blocks, :] = first[pl.ds(8 + i, 2 * blocks, stride=tall), :]
        halo_out[0, i, 0 : 2 * blocks, :] = first[
            pl.ds(8 + rows - HALO + i, 2 * blocks, stride=tall), :
        ]

    upward = remote(
        halo_out.at[1], halo.at[1], halo_sends.at[1], halo_recvs.at[1], {"tile": tile - 1}
    )
    downward = remote(
        halo_out.at[0], halo.at[0], halo_sends.at[0], halo_recvs.at[0], {"tile": tile + 1}
    )

    def put_halo(side, from_halo):
        for i in range(HALO):
            at = 8 - HALO + i if side == 0 else 8 + rows + i
            value = halo[side, i, 0 : 2 * blocks, :]
            if not from_halo:
                value = jnp.zeros_like(value)
            first[pl.ds(at, 2 * blocks, stride=tall), :] = value

    @pl.when(tile > 0)
    def _():
        upward.start()

    @pl.when(tile < n - 1)
    def _():
        downward.start()

    @pl.when(tile > 0)
    def _():
        downward.wait_recv()
        put_halo(0, True)

    @pl.when(tile == 0)
    def _():
        put_halo(0, False)

    @pl.when(tile < n - 1)
    def _():
        upward.wait_recv()
        put_halo(1, True)

    @pl.when(tile == n - 1)
    def _():
        put_halo(1, False)

    row = tile * rows - 8 + lax.broadcasted_iota(jnp.int32, (tall, 128), 0)
    line = lax.broadcasted_iota(jnp.int32, (1, 128), 1)
    tall_lane = lax.broadcasted_iota(jnp.int32, (tall, 128), 1)
    row_inside = (row >= 0) & (row < n * rows)
    row_down = (row >= 0) & (row < n * rows - 1)

    def sweep(source, write):
        field = [[source[tall * (p * blocks + k) : tall * (p * blocks + k + 1), :] for k in range(blocks)] for p in range(2)]
        down = [[], []]
        right = [[], []]
        for k in range(blocks):
            column = (group * share + k) * 128 + line
            if k == share:
                column = jnp.where(line < 64, column, column - 128 * blocks)
            column_inside = (column >= 0) & (column < NCOL)
            column_right = (column >= 0) & (column < NCOL - 1)
            square = floor_square
            for p in range(2):
                here = field[p][k]
                following = field[p][(k + 1) % blocks]
                beside = pltpu.roll(jnp.where(tall_lane == 0, following, here), 127, 1)
                below = pltpu.roll(here, tall - 1, 0)
                down[p].append(jnp.where(row_down & column_inside, below - here, 0.0))
                right[p].append(jnp.where(row_inside & column_right, beside - here, 0.0))
                square = square + (down[p][k] * down[p][k] + right[p][k] * right[p][k])
            inverse = lax.rsqrt(square)
            for p in range(2):
                down[p][k] = down[p][k] * inverse
                right[p][k] = right[p][k] * inverse
        for p in range(2):
            for k in range(blocks):
                before = right[p][(k - 1) % blocks]
                left = pltpu.roll(jnp.where(tall_lane == 127, before, right[p][k]), 1, 1)
                above = pltpu.roll(down[p][k], 1, 0)
                divergence = down[p][k] - above + right[p][k] - left
                at = tall * (p * blocks + k)
                here = field[p][k]
                base = first[at : at + tall, :]
                write(p, k, here - step_size * (here - base - tv_weight * divergence))

    def write_second(p, k, value):
        at = tall * (p * blocks + k)
        second[at : at + tall, :] = value

    def write_out(p, k, value):
        if k < share:
            out_ref[p, :, 128 * k : 128 * (k + 1)] = value[8 : 8 + rows]

    sweep(first, write_second)
    sweep(second, write_out)

    @pl.when(tile > 0)
    def _():
        upward.wait_send()

    @pl.when(tile < n - 1)
    def _():
        downward.wait_send()

    def sent(d, c):
        block_copy(d).wait_send()
        value_copy(d).wait_send()
        return c

    lax.fori_loop(1, half, sent, 0)
    for copy in infos:
        copy.wait_send()
    cross.wait_send()
    for strip in (NEAR, FAR):
        for d in range(1, groups):
            for side in range(2):
                part_copy(strip, d, side).wait_send()


def body(echoes, pulse_slope, pulse_shift, footprint, band_start, row_phase):
    n = lax.axis_size("tile")
    groups = lax.axis_size("pulse")
    held, pulses = pulse_slope.shape
    rows = band_start.shape[0]
    bins = echoes.shape[3] // 128
    planes = 2 * pulses
    share = KBLOCKS // groups
    planes_of = echoes.reshape(held, planes * bins, 128)
    table = jnp.asarray(interpolation_table(), BF16)

    vmem = pl.BlockSpec(memory_space=pltpu.VMEM)
    anywhere = pl.BlockSpec(memory_space=pl.ANY)
    blocks = share + 1
    edge_rows = 8 * (-(-2 * blocks // 8))
    value_rows = 8 * (-(-held * planes // 8))
    field = (2 * blocks * (rows + 16), 128)
    piece = (2, blocks * rows, 128)
    dma = pltpu.SemaphoreType.DMA
    refined = pl.pallas_call(
        functools.partial(kernel, held, pulses, rows, groups, n),
        out_shape=jax.ShapeDtypeStruct((2, rows, 128 * share), F32),
        in_specs=[anywhere] * 7,
        out_specs=vmem,
        scratch_shapes=[
            pltpu.SMEM(footprint.shape, jnp.int32),
            pltpu.VMEM((1, rows), jnp.int32),
            pltpu.SMEM((2, 1, rows), jnp.int32),
            pltpu.VMEM(pulse_slope.shape, BF16),
            pltpu.VMEM(pulse_shift.shape, BF16),
            pltpu.VMEM((2, 1, rows), F32),
            pltpu.VMEM((2, rows, 128), F32),
            pltpu.VMEM(table.shape, BF16),
            pltpu.VMEM((value_rows, 128), F32),
            pltpu.VMEM((n // 2, value_rows, 128), F32),
            pltpu.VMEM((n // 2,) + planes_of.shape, BF16),
            pltpu.VMEM((planes, bins + 8, 128), F32),
            pltpu.VMEM((2, planes * 64, 512), BF16),
            pltpu.VMEM((2, planes * 64, 512), F32),
            pltpu.VMEM((pulses, 2, 4, 8, 128), F32),
            pltpu.VMEM((pulses, 2, rows, 128), F32),
            pltpu.VMEM((4 * rows * KBLOCKS, 128), F32),
            pltpu.VMEM((2, groups) + piece, BF16),
            pltpu.VMEM((2, groups - 1) + piece, BF16),
            pltpu.VMEM(piece, BF16),
            pltpu.VMEM(piece, BF16),
            pltpu.VMEM(field, F32),
            pltpu.VMEM(field, F32),
            pltpu.VMEM((2, HALO, edge_rows, 128), F32),
            pltpu.VMEM((2, HALO, edge_rows, 128), F32),
            dma((7,)),
            dma((2,)),
            dma((2,)),
            dma((n // 2,)),
            dma((n // 2,)),
            dma((n // 2,)),
            dma((n // 2,)),
            dma((2, groups - 1, 2)),
            dma((2, groups - 1, 2)),
            dma((1,)),
            dma((1,)),
            dma((2,)),
            dma((2,)),
        ],
        compiler_params=pltpu.CompilerParams(
            collective_id=0, has_side_effects=True, vmem_limit_bytes=60 * 1024 * 1024
        ),
    )(
        footprint,
        band_start.reshape(1, rows),
        planes_of,
        pulse_slope,
        pulse_shift,
        row_phase.reshape(1, rows),
        table,
    )
    return refined


def solution(mesh):
    in_specs = (
        P(("pulse", "tile"), None, None, None),
        P(("pulse", "tile"), None),
        P(("pulse", "tile"), None),
        P("pulse", None, None),
        P("tile"),
        P("tile"),
    )
    out_specs = P(None, "tile", "pulse")
    return jax.shard_map(body, mesh=mesh, in_specs=in_specs, out_specs=out_specs, check_vma=False)
```
